32 devices in a mesh: fsdp: 16 (over z, x, core), island: 2 (over y).
Axes of the slice: x: 2, y: 2, z: 4, core: 2. Of those that a mesh axis runs over, the one named last changes fastest.
Arguments:
- activations: bfloat16 [2, 2048, 4224], P('island', 'fsdp'), may hold values from -6 to 6
- out_grads: bfloat16 [2, 2048, 512], P('island', 'fsdp'), may hold values from -0.13183594 to 0.13183594
- projection: bfloat16 [4224, 256], P('fsdp'), may hold values from -0.09375 to 0.09375
- first_moment: float32 [2, 1, 256, 512], P('island'), may hold values from -1.8 to 1.8
- second_moment: float32 [2, 1, 256, 512], P('island'), may hold values from 0.01 to 1
- inner_weights: float32 [2, 4224, 512], P('island', 'fsdp'), may hold values from -6 to 6
- global_weights: float32 [4224, 512], P('fsdp'), may hold values from -6 to 6
- outer_momentum: float32 [4224, 512], P('fsdp'), may hold values from -6 to 6
Outputs:
- new_weights: bfloat16 [4224, 512], P('fsdp', 'island')
- new_momentum: float32 [4224, 512], P('fsdp')
- new_first: float32 [2, 1, 256, 512], P('island')
- new_second: float32 [2, 1, 256, 512], P('island')
The draws below stay inside these ranges and needn't reach their ends.
All inputs are finite; a program needn't handle non-finite values.
Results may differ from the reference program's by a relative error of at most 0.001.
Values sent between devices are 32-bit elements; how exact they have to be, the bound alone decides.
No kernel may reach another device: no remote copies, remote signals or barrier semaphores. Data moves between devices by JAX's collectives and lax.ppermute only.
A program may use at most 64 MiB of HBM per device.

```python
import math
import jax
import jax.numpy as jnp
from jax import lax

DW = 4224
COLS = 512
RANK = 256
LAYERS = 1
TOKENS = 2048
ROWS = 4224
N_ISLAND = 2


def raised(values, stream_key, source, target, shards_of, factor):
    def block_of(dim):
        return (jnp.arange(values.shape[dim]) // (values.shape[dim] // shards_of)).reshape((-1,) + (1,) * (values.ndim - 1 - dim))

    one_side = jax.random.permutation(stream_key, shards_of)[block_of(target)]
    other_side = (block_of(target) + shards_of // 2) % shards_of
    return jnp.where((block_of(source) == one_side) | (block_of(source) == other_side), factor * values, values)


def block_scale(own_key, extent, cuts, smallest, largest):
    level, own = 1.0, jax.random.fold_in(own_key, 6)
    for axis_at, parts in cuts:
        steps = jnp.exp(jax.random.uniform(jax.random.fold_in(own, axis_at), (parts,), jnp.float32, smallest / len(cuts), largest / len(cuts)))
        level = level * jnp.repeat(steps, extent[axis_at] // parts).reshape([-1 if axis == axis_at else 1 for axis in range(len(extent))])
    return level


def bell_draw(rng, shape, width, most, shards=(), kind=jnp.bfloat16):
    drawn = width * jax.random.normal(rng, shape, jnp.float32)
    if shards:
        drawn = drawn * block_scale(rng, shape, shards, -0.22, 0.18)
    return jnp.clip(drawn, -most, most).astype(kind)


def gaussian_with(rng, shape, spread, limit, cuts, heavy, kind=jnp.bfloat16):
    drawn = spread * jax.random.normal(rng, shape, jnp.float32)
    if cuts:
        drawn = drawn * block_scale(rng, shape, cuts, -0.22, 0.18)
    return jnp.clip(raised(drawn, jax.random.fold_in(rng, 3), *heavy), -limit, limit).astype(kind)


def setup_inputs(seed: int = 0) -> dict:
    arg_keys = jax.random.split(jax.random.key(seed), 9)
    activations = gaussian_with(arg_keys[0], (N_ISLAND, TOKENS, ROWS), 1.0, 6.0, ((0, 2), (1, 16)), (1, 2, 16, 2.0))
    out_grads = bell_draw(arg_keys[1], (N_ISLAND, TOKENS, LAYERS * COLS), (TOKENS ** -0.5), 0.13183594, ((0, 2), (1, 16)))
    projection = bell_draw(arg_keys[2], (ROWS, RANK), DW ** -0.5, 0.09375, ((0, 16),))
    first_moment = bell_draw(arg_keys[3], (N_ISLAND, LAYERS, RANK, COLS), 0.3, 1.8, ((0, 2),), jnp.float32)
    second_moment = jnp.clip(jnp.exp(math.log(1.0) - 4.6051702 * jax.random.uniform(arg_keys[4], (N_ISLAND, LAYERS, RANK, COLS), jnp.float32) ** block_scale(arg_keys[4], (N_ISLAND, LAYERS, RANK, COLS), ((0, 2),), -0.2, 0.2)), 0.01, 1.0)
    inner_weights = bell_draw(arg_keys[5], (N_ISLAND, ROWS, COLS), 1.0, 6.0, ((0, 2), (1, 16)), jnp.float32)
    global_weights = bell_draw(arg_keys[6], (ROWS, COLS), 1.0, 6.0, ((0, 16),), jnp.float32)
    outer_momentum = bell_draw(arg_keys[7], (ROWS, COLS), 1.0, 6.0, ((0, 16),), jnp.float32)
    return {"activations": activations, "out_grads": out_grads, "projection": projection, "first_moment": first_moment, "second_moment": second_moment, "inner_weights": inner_weights, "global_weights": global_weights, "outer_momentum": outer_momentum}


first_decay = 0.9
second_decay = 0.999
first_fix = 1.0 - 0.9 ** 10
second_fix = 1.0 - 0.999 ** 10
epsilon = 1e-08
inner_rate = 1.0
outer_rate = 0.7
outer_beta = 0.9

def reference(activations, out_grads, projection, first_moment, second_moment, inner_weights, global_weights, outer_momentum):
    stepped_list = []
    first_list = []
    second_list = []
    for island_index in range(N_ISLAND):
        inputs = activations[island_index]
        grads_out = out_grads[island_index]
        pieces = []
        projected_list = []
        for layer_index in range(LAYERS):
            block = inputs[:, layer_index * DW:(layer_index + 1) * DW]
            grad_block = grads_out[:, layer_index * COLS:(layer_index + 1) * COLS]
            gradient = jnp.dot(block.T, grad_block, preferred_element_type=jnp.float32)
            pieces.append(gradient)
            proj_block = projection[layer_index * DW:(layer_index + 1) * DW].astype(jnp.float32)
            projected_list.append(jnp.dot(proj_block.T, gradient, precision=lax.Precision.HIGHEST))
        gradient_all = jnp.concatenate(pieces, axis=0)
        projected = jnp.stack(projected_list)
        new_first = first_decay * first_moment[island_index] + (1.0 - first_decay) * projected
        new_second = second_decay * second_moment[island_index] + (1.0 - second_decay) * projected * projected
        adapted = new_first / first_fix / (jnp.sqrt(new_second / second_fix) + epsilon)
        channel_scale = jnp.sqrt(lax.optimization_barrier(jnp.mean(adapted * adapted, axis=1))) / jnp.sqrt(lax.optimization_barrier(jnp.mean(projected * projected, axis=1)) + 1e-06)
        row_scale = jnp.repeat(channel_scale, DW, axis=0)
        stepped_list.append(inner_weights[island_index] - inner_rate * gradient_all * row_scale)
        first_list.append(new_first)
        second_list.append(new_second)
    island_total = stepped_list[0]
    for island_index in range(1, N_ISLAND):
        island_total = island_total + stepped_list[island_index]
    pseudo_grad = global_weights - island_total / N_ISLAND
    new_momentum = outer_beta * outer_momentum + pseudo_grad
    new_weights = (global_weights - outer_rate * (pseudo_grad + outer_beta * new_momentum)).astype(jnp.bfloat16)
    return (new_weights, new_momentum, jnp.stack(first_list), jnp.stack(second_list))
```

```python
import jax
import jax.numpy as jnp
from jax import lax
from jax.experimental import pallas as pl
from jax.experimental.pallas import tpu as pltpu
from jax.sharding import PartitionSpec as P

first_decay = 0.9
second_decay = 0.999
first_fix = 1.0 - 0.9**10
second_fix = 1.0 - 0.999**10
epsilon = 1e-08
inner_rate = 1.0
outer_rate = 0.7
outer_beta = 0.9


def outer_step(stepped_sum, global_part, momentum_part, island_count):
    pseudo_grad = global_part - stepped_sum / island_count
    momentum_next = outer_beta * momentum_part + pseudo_grad
    weights_next = (global_part - outer_rate * (pseudo_grad + outer_beta * momentum_next)).astype(
        jnp.bfloat16
    )
    return (weights_next, momentum_next)


def moments_and_scale(projected, first, second):
    new_first = first_decay * first + (1.0 - first_decay) * projected
    new_second = second_decay * second + (1.0 - second_decay) * projected * projected
    adapted = new_first / first_fix / (jnp.sqrt(new_second / second_fix) + epsilon)
    scale = jnp.sqrt(jnp.mean(adapted * adapted, axis=0, keepdims=True)) / jnp.sqrt(
        jnp.mean(projected * projected, axis=0, keepdims=True) + 1e-06
    )
    return new_first, new_second, scale


def plain_body(
    activations,
    out_grads,
    projection,
    first_moment,
    second_moment,
    inner_weights,
    global_weights,
    outer_momentum,
):
    col_total = global_weights.shape[1]
    product = lax.dot_general(
        activations[0],
        out_grads[0],
        (((0,), (0,)), ((), ())),
        preferred_element_type=jnp.float32,
    )
    grad_rows = lax.psum_scatter(product, "fsdp", scatter_dimension=0, tiled=True)
    partial_sum = lax.dot_general(
        projection.astype(jnp.float32),
        grad_rows,
        (((0,), (0,)), ((), ())),
        precision=lax.Precision.HIGHEST,
        preferred_element_type=jnp.float32,
    )
    projected = lax.psum(partial_sum, "fsdp")
    new_first, new_second, scale = moments_and_scale(
        projected, first_moment[0, 0], second_moment[0, 0]
    )
    stepped = inner_weights[0] - inner_rate * grad_rows * scale
    island_count = lax.axis_size("island")
    block_cols = col_total // island_count
    block_start = lax.axis_index("island") * block_cols
    share_total = lax.psum_scatter(stepped, "island", scatter_dimension=1, tiled=True)
    global_part = lax.dynamic_slice_in_dim(global_weights, block_start, block_cols, 1)
    momentum_part = lax.dynamic_slice_in_dim(outer_momentum, block_start, block_cols, 1)
    weights_block, momentum_block = outer_step(
        share_total, global_part, momentum_part, island_count
    )
    new_momentum = lax.all_gather(momentum_block, "island", axis=1, tiled=True)
    return (weights_block, new_momentum, new_first[None, None], new_second[None, None])


def product_kernel(
    at, own_a, core_a, crossed_a, own_g, core_g, side_g, far_g, out
):
    pieces = (
        (own_a[0, 0], own_g),
        (core_a[0, 0], core_g),
        (crossed_a[0], side_g),
        (crossed_a[1], far_g),
    )
    out[...] = sum(
        jnp.dot(
            a.astype(jnp.bfloat16),
            g[...].astype(jnp.bfloat16),
            preferred_element_type=jnp.float32,
        )
        for a, g in pieces
    )


def block_product(at, own_a, core_a, crossed_a, grads):
    rows, tokens = own_a.shape[2:]
    cols = grads[0].shape[1]
    picked = pl.BlockSpec((1, 1, rows, tokens), lambda i, at: (at[0], at[1], 0, 0))
    whole = pl.BlockSpec((tokens, cols), lambda i, at: (0, 0))
    return pl.pallas_call(
        product_kernel,
        out_shape=jax.ShapeDtypeStruct((rows, cols), jnp.float32),
        grid_spec=pltpu.PrefetchScalarGridSpec(
            num_scalar_prefetch=1,
            grid=(1,),
            in_specs=[
                picked,
                picked,
                pl.BlockSpec((2, rows, tokens), lambda i, at: (0, 0, 0)),
                whole,
                whole,
                whole,
                whole,
            ],
            out_specs=pl.BlockSpec((rows, cols), lambda i, at: (0, 0)),
        ),
        compiler_params=pltpu.CompilerParams(vmem_limit_bytes=24 * 1024 * 1024),
        cost_estimate=pl.CostEstimate(
            flops=8 * rows * tokens * cols,
            bytes_accessed=4 * (4 * tokens * (rows + cols) + rows * cols),
            transcendentals=0,
        ),
    )(at, own_a, core_a, crossed_a, *grads)


def line_body(
    activations,
    out_grads,
    projection,
    first_moment,
    second_moment,
    inner_weights,
    global_weights,
    outer_momentum,
):
    fsdp = lax.axis_size("fsdp")
    line = fsdp // 4
    me = lax.axis_index("fsdp")
    place, side, core = me // 4, (me // 2) % 2, me % 2
    at_end = (place == 0) | (place == line - 1)
    rows = projection.shape[0]
    tokens, features = activations.shape[1:]
    cols = global_weights.shape[1]
    rank = projection.shape[1]

    def move(value, target):
        pairs = []
        for f in range(fsdp):
            to = target(f // 4, (f // 2) % 2, f % 2)
            if to is not None:
                pairs.append((f, (to[0] * 2 + to[1]) * 2 + to[2]))
        return lax.ppermute(value, "fsdp", pairs)

    def to_core(value):
        return move(value, lambda l, x, c: (l, x, 1 - c))

    def to_side(value):
        return move(value, lambda l, x, c: (l, 1 - x, c))

    def to_place(value, mask):
        return move(value, lambda l, x, c: (l ^ mask, x, c))

    def inward(value, depth):
        def target(l, x, c):
            if l == depth:
                return (l + 1, x, c)
            if l == line - 1 - depth:
                return (l - 1, x, c)
            return None

        return move(value, target)

    def to_island(value):
        return lax.ppermute(value, "island", [(0, 1), (1, 0)])

    grads_own = out_grads[0].astype(jnp.float32)
    grads_side = to_side(grads_own)

    turned = lax.dot_general(
        activations[0],
        jnp.eye(tokens, dtype=activations.dtype),
        (((0,), (0,)), ((), ())),
        preferred_element_type=jnp.float32,
    ).reshape(line, 2, 2, rows, tokens)
    kept = lax.dynamic_index_in_dim(turned, core, 2, keepdims=False)
    from_core = to_core(lax.dynamic_index_in_dim(turned, 1 - core, 2, keepdims=False))
    grads_core = to_core(grads_own)
    grads_far = to_core(grads_side)

    table = []
    for l in range(line):
        needed = []
        for b in range(line):
            depth, hops = (l, b - l) if b > l else (line - 1 - l, l - b)
            needed.append((line - hops if hops else line + 1, depth, b))
        table.append([b for _, _, b in sorted(needed)])
    order = jnp.array(table, jnp.int32)[place]

    def block(stack, k, which):
        return lax.dynamic_slice(stack, (order[k], which, 0, 0), (1, 1, rows, tokens))[0, 0]

    proj_own = projection.astype(jnp.float32)
    proj_in = inward(proj_own, 0)
    proj_mid = inward(proj_own, 1)
    proj_mid2 = inward(proj_in, 1)
    proj_out = inward(jnp.stack([proj_own, proj_mid]), 2)
    proj_out2 = inward(proj_mid2, 2)
    proj_order = [
        jnp.where(at_end, proj_out2, proj_mid2),
        jnp.where(at_end, proj_out[1], proj_mid),
        jnp.where(at_end, proj_out[0], proj_in),
        proj_own,
    ]

    grads = (grads_own, grads_core, grads_side, grads_far)
    products = []
    for k in range(line):
        crossed = to_side(
            jnp.stack([block(kept, k, 1 - side), block(from_core, k, 1 - side)])
        )
        at = jnp.stack([order[k], side]).astype(jnp.int32)
        products.append(block_product(at, kept, from_core, crossed, grads))

    e1 = inward(products[0], 0)
    m1 = inward(products[0] + e1, 1)
    e2 = inward(products[1], 0)
    m2 = inward(products[1] + e2, 1)
    o1 = inward(products[2] + m1, 2)
    e3 = inward(products[2], 0)
    grad_rows = products[3] + e3 + m2 + o1

    partial = sum(
        lax.dot_general(
            products[k],
            proj_order[k],
            (((0,), (0,)), ((), ())),
            precision=lax.Precision.HIGH,
            preferred_element_type=jnp.float32,
        )
        for k in range(line)
    )

    def halve(value, bit, exchange):
        half = value.shape[0] // 2
        mine = lax.dynamic_slice_in_dim(value, bit * half, half, 0)
        other = lax.dynamic_slice_in_dim(value, (1 - bit) * half, half, 0)
        return mine + exchange(other)

    def double(value, bit, exchange):
        other = exchange(value)
        return jnp.where(
            bit == 0,
            jnp.concatenate([value, other]),
            jnp.concatenate([other, value]),
        )

    stages = (
        (core, to_core),
        (side, to_side),
        (place // 2, lambda v: to_place(v, 2)),
        (place % 2, lambda v: to_place(v, 1)),
    )
    for bit, exchange in stages:
        partial = halve(partial, bit, exchange)
    for bit, exchange in reversed(stages):
        partial = double(partial, bit, exchange)
    projected = partial.T

    new_first, new_second, scale = moments_and_scale(
        projected, first_moment[0, 0], second_moment[0, 0]
    )

    island = lax.axis_index("island")

    def ordered(own, other):
        return jnp.where(island == 0, own, other), jnp.where(island == 0, other, own)

    inner = inner_weights[0]
    inner0, inner1 = ordered(inner, to_island(inner))
    grad0, grad1 = ordered(grad_rows, to_island(grad_rows))
    scale0, scale1 = ordered(scale, to_island(scale))
    total = (inner0 - inner_rate * grad0 * scale0) + (inner1 - inner_rate * grad1 * scale1)
    weights, new_momentum = outer_step(total, global_weights, outer_momentum, 2)
    half_cols = cols // 2
    weights_block = lax.dynamic_slice_in_dim(weights, island * half_cols, half_cols, 1)
    return (weights_block, new_momentum, new_first[None, None], new_second[None, None])


def solution(mesh):
    placed = (
        P("island", "fsdp", None),
        P("island", "fsdp", None),
        P("fsdp", None),
        P("island", None, None, None),
        P("island", None, None, None),
        P("island", "fsdp", None),
        P("fsdp", None),
        P("fsdp", None),
    )
    lined = mesh.shape["fsdp"] == 4 * 4 and mesh.shape["island"] == 2
    return jax.shard_map(
        line_body if lined else plain_body,
        mesh=mesh,
        in_specs=placed,
        out_specs=(
            P("fsdp", "island"),
            P("fsdp", None),
            P("island", None, None, None),
            P("island", None, None, None),
        ),
        check_vma=False,
    )
```

```python
import jax
import jax.numpy as jnp
from jax import lax
from jax.experimental import pallas as pl
from jax.experimental.pallas import tpu as pltpu
from jax.sharding import PartitionSpec as P

first_decay = 0.9
second_decay = 0.999
first_fix = 1.0 - 0.9**10
second_fix = 1.0 - 0.999**10
epsilon = 1e-08
inner_rate = 1.0
outer_rate = 0.7
outer_beta = 0.9


def outer_step(stepped_sum, global_part, momentum_part, island_count):
    pseudo_grad = global_part - stepped_sum / island_count
    momentum_next = outer_beta * momentum_part + pseudo_grad
    weights_next = (global_part - outer_rate * (pseudo_grad + outer_beta * momentum_next)).astype(
        jnp.bfloat16
    )
    return (weights_next, momentum_next)


def moments_and_scale(projected, first, second):
    new_first = first_decay * first + (1.0 - first_decay) * projected
    new_second = second_decay * second + (1.0 - second_decay) * projected * projected
    adapted = new_first / first_fix / (jnp.sqrt(new_second / second_fix) + epsilon)
    scale = jnp.sqrt(jnp.mean(adapted * adapted, axis=0, keepdims=True)) / jnp.sqrt(
        jnp.mean(projected * projected, axis=0, keepdims=True) + 1e-06
    )
    return new_first, new_second, scale


def plain_body(
    activations,
    out_grads,
    projection,
    first_moment,
    second_moment,
    inner_weights,
    global_weights,
    outer_momentum,
):
    col_total = global_weights.shape[1]
    product = lax.dot_general(
        activations[0],
        out_grads[0],
        (((0,), (0,)), ((), ())),
        preferred_element_type=jnp.float32,
    )
    grad_rows = lax.psum_scatter(product, "fsdp", scatter_dimension=0, tiled=True)
    partial_sum = lax.dot_general(
        projection.astype(jnp.float32),
        grad_rows,
        (((0,), (0,)), ((), ())),
        precision=lax.Precision.HIGHEST,
        preferred_element_type=jnp.float32,
    )
    projected = lax.psum(partial_sum, "fsdp")
    new_first, new_second, scale = moments_and_scale(
        projected, first_moment[0, 0], second_moment[0, 0]
    )
    stepped = inner_weights[0] - inner_rate * grad_rows * scale
    island_count = lax.axis_size("island")
    block_cols = col_total // island_count
    block_start = lax.axis_index("island") * block_cols
    share_total = lax.psum_scatter(stepped, "island", scatter_dimension=1, tiled=True)
    global_part = lax.dynamic_slice_in_dim(global_weights, block_start, block_cols, 1)
    momentum_part = lax.dynamic_slice_in_dim(outer_momentum, block_start, block_cols, 1)
    weights_block, momentum_block = outer_step(
        share_total, global_part, momentum_part, island_count
    )
    new_momentum = lax.all_gather(momentum_block, "island", axis=1, tiled=True)
    return (weights_block, new_momentum, new_first[None, None], new_second[None, None])


VMEM_BYTES = 32 * 1024 * 1024


def whole_block(shape):
    return pl.BlockSpec(shape, lambda *_: (0,) * len(shape))


def run(kernel, out_shapes, args, after=(), scalars=None, blocks=None, scratch=()):
    blocks = blocks or {}
    lead = 0 if scalars is None else 1
    ins = lead + len(args)

    def body(*refs):
        kernel(*refs[:ins], *refs[ins + len(after) :])

    return pl.pallas_call(
        body,
        out_shape=[jax.ShapeDtypeStruct(shape, kind) for shape, kind in out_shapes],
        grid_spec=pltpu.PrefetchScalarGridSpec(
            num_scalar_prefetch=lead,
            grid=(1,),
            in_specs=[blocks.get(i, whole_block(arg.shape)) for i, arg in enumerate(args)]
            + [pl.BlockSpec(memory_space=pl.ANY)] * len(after),
            out_specs=[whole_block(shape) for shape, _ in out_shapes],
            scratch_shapes=scratch,
        ),
        compiler_params=pltpu.CompilerParams(vmem_limit_bytes=VMEM_BYTES),
        cost_estimate=pl.CostEstimate(flops=0, bytes_accessed=0, transcendentals=0),
    )(*(() if scalars is None else (scalars,)), *args, *after)


F32 = jnp.float32
BF16 = jnp.bfloat16


def turn_kernel(at, a_ref, g_ref, first, far, rest, here, cores, turned):
    tokens, features = a_ref.shape[1:]
    cols = g_ref.shape[2]
    line, rows = here.shape[:2]
    for at_col in range(0, features, tokens):
        turned[at_col : at_col + tokens, :] = (
            a_ref[0, :, at_col : at_col + tokens].astype(F32).T
        )
    for at_col in range(0, cols, tokens):
        first[at_col : at_col + tokens, :] = g_ref[0, :, at_col : at_col + tokens].astype(F32)
    side, core = at[line], at[line + 1]

    def block(k, toward, which):
        start = pl.multiple_of(((at[k] * 2 + toward) * 2 + which) * rows, 8)
        return turned[pl.ds(start, rows), :]

    first[cols:, :] = block(0, 1 - side, core)
    far[...] = block(0, 1 - side, 1 - core)
    for k in range(line):
        here[k] = block(k, side, core)
        cores[k] = block(k, side, 1 - core)
        if k:
            rest[k - 1] = block(k, 1 - side, core)
            cores[line + k - 1] = block(k, 1 - side, 1 - core)


def pair_kernel(*refs):
    out = refs[-1]
    for i, ref in enumerate(refs[:-1]):
        out[i % 2, i // 2] = ref[...]


def stack_kernel(*refs):
    for i, ref in enumerate(refs[:-1]):
        refs[-1][i] = ref[...]


def gather_kernel(near, away, out):
    out[0] = near[...]
    out[1:] = away[...]


def half_kernel(flag, value, out):
    half = out.shape[1]
    out[...] = jnp.where(
        flag[:, :half] == 0, value[:, :half].astype(F32), value[:, half:].astype(F32)
    )


def two_kernel(g_ref, crossed, out):
    tokens = g_ref.shape[1]
    cols = g_ref.shape[2]
    for at_col in range(0, cols, tokens):
        out[0, at_col : at_col + tokens, :] = g_ref[0, :, at_col : at_col + tokens].astype(F32)
    out[1] = crossed[:cols, :]


def first_product_kernel(here, core_a, crossed, far, g_ref, core_g, out, grads):
    tokens = g_ref.shape[1]
    cols = g_ref.shape[2]
    grads[:tokens, :] = g_ref[0]
    for at_col in range(0, cols, tokens):
        span = slice(at_col, at_col + tokens)
        grads[tokens : 2 * tokens, span] = core_g[0, span, :].astype(BF16)
        grads[2 * tokens : 3 * tokens, span] = crossed[span, :].astype(BF16)
        grads[3 * tokens :, span] = core_g[1, span, :].astype(BF16)
    pieces = (here[0], core_a[0], crossed[cols:, :], far[...])
    a = jnp.concatenate([piece.astype(BF16) for piece in pieces], axis=1)
    out[...] = jnp.dot(a, grads[...], preferred_element_type=F32)


def product_kernel(here, core_a, grads, *refs):
    outs = refs[len(refs) - (here.shape[0] - 1) :]
    crossed = [(ref, i) for ref in refs[: -len(outs)] for i in range(ref.shape[1])]
    for k, (out, (ref, i)) in enumerate(zip(outs, crossed)):
        pieces = (here[k + 1], core_a[k + 1], ref[0, i], ref[1, i])
        a = jnp.concatenate([piece.astype(BF16) for piece in pieces], axis=1)
        out[...] = jnp.dot(a, grads[...], preferred_element_type=F32)


def sum_kernel(*refs):
    total = refs[0][...]
    for ref in refs[1:-1]:
        total = total + ref[...]
    refs[-1][...] = total


def lift_kernel(flag, p0, p1, p2, p3, own, received, others, out):
    half = others.shape[2]
    first = flag[:, :half] == 0
    low, high = own[:, :half].astype(F32), own[:, half:].astype(F32)
    mine = (received[2], received[0], received[1], jnp.where(first, low, high))
    theirs = (others[2], others[0], others[1], jnp.where(first, high, low))
    splits = []
    for product in (p0, p1, p2, p3):
        value = product[...]
        top = value.astype(BF16)
        splits.append((top, (value - top.astype(F32)).astype(BF16)))
    totals = []
    for rows in (mine, theirs):
        total = None
        for row, parts in zip(rows, splits):
            turned = row.T.astype(BF16)
            for part in parts:
                term = jnp.dot(turned, part, preferred_element_type=F32)
                total = term if total is None else total + term
        totals.append(total)
    first = flag[...] == 0
    out[:half, :] = jnp.where(first, totals[0], totals[1])
    out[half:, :] = jnp.where(first, totals[1], totals[0])


def outer_kernel(
    flag, inner_sum, grad, grad_other, scale, scale_other, weights, momentum, out, momentum_out
):
    first_island = flag[...] == 0
    own, other = grad[...] * scale[...], grad_other[...] * scale_other[...]
    first, second = jnp.where(first_island, own, other), jnp.where(first_island, other, own)
    total = (inner_sum[...] - inner_rate * first) - inner_rate * second
    weights_next, momentum_next = outer_step(total, weights[...], momentum[...], 2)
    half = out.shape[1]
    out[...] = jnp.where(
        flag[:, :half] == 0,
        weights_next[:, :half].astype(F32),
        weights_next[:, half:].astype(F32),
    ).astype(BF16)
    momentum_out[...] = momentum_next


def line_body(
    activations,
    out_grads,
    projection,
    first_moment,
    second_moment,
    inner_weights,
    global_weights,
    outer_momentum,
):
    fsdp = lax.axis_size("fsdp")
    line = fsdp // 4
    me = lax.axis_index("fsdp")
    place, side, core = me // 4, (me // 2) % 2, me % 2
    rows = projection.shape[0]
    tokens, features = activations.shape[1:]
    cols = global_weights.shape[1]
    rank = projection.shape[1]

    def move(value, target):
        pairs = []
        for f in range(fsdp):
            to = target(f // 4, (f // 2) % 2, f % 2)
            if to is not None:
                pairs.append((f, (to[0] * 2 + to[1]) * 2 + to[2]))
        return lax.ppermute(value, "fsdp", pairs)

    def to_core(value):
        return move(value, lambda l, x, c: (l, x, 1 - c))

    def to_side(value):
        return move(value, lambda l, x, c: (l, 1 - x, c))

    def to_far(value):
        return move(value, lambda l, x, c: (l, 1 - x, 1 - c))

    def to_place(value, mask):
        return move(value, lambda l, x, c: (l ^ mask, x, c))

    def to_island(value):
        return lax.ppermute(value, "island", [(0, 1), (1, 0)])

    island = lax.axis_index("island")
    at = jnp.stack([place ^ 3, place ^ 1, place ^ 2, place, side, core]).astype(jnp.int32)
    flag = jnp.full((1, cols), island, F32)

    block_shape = (rows, tokens)
    first, far, rest, here, cores = run(
        turn_kernel,
        [
            ((cols + rows, tokens), F32),
            (block_shape, F32),
            ((line - 1, *block_shape), F32),
            ((line, *block_shape), F32),
            ((2 * line - 1, *block_shape), F32),
        ],
        [activations, out_grads],
        scalars=at,
        scratch=[pltpu.VMEM((features, tokens), F32)],
    )
    first = to_side(first)
    far = to_far(far)
    from_core = to_core(cores)

    def blocks_of(start, count):
        return pl.BlockSpec((count, *block_shape), lambda *_: (start // count, 0, 0))

    def cross(k, count, after):
        parts = []
        for i in range(count):
            parts += [rest[k - 1 + i], from_core[line + k - 1 + i]]
        (paired,) = run(
            pair_kernel, [((2, count, *block_shape), F32)], parts, after=after
        )
        return to_side(paired)

    def total(*terms, after=()):
        return run(sum_kernel, [(terms[0].shape, F32)], terms, after=after)[0]

    half_rank = (rows, rank // 2)
    (proj_half,) = run(half_kernel, [(half_rank, F32)], [flag, projection])
    proj_near = to_place(proj_half, 1)
    (proj_two,) = run(stack_kernel, [((2, *half_rank), F32)], [proj_half, proj_near])
    proj_away = to_place(proj_two, 2)
    (grads_two,) = run(
        two_kernel, [((2, cols, tokens), F32)], [out_grads, first], after=[far]
    )
    grads_core = to_core(grads_two)
    (proj_stack,) = run(
        gather_kernel, [((3, *half_rank), F32)], [proj_near, proj_away], after=[grads_two]
    )
    proj_others = to_island(proj_stack)
    crossed = [cross(1, 1, [grads_two]), cross(2, line - 2, [grads_two])]
    product0, grads = run(
        first_product_kernel,
        [((rows, cols), F32), ((4 * tokens, cols), BF16)],
        [here, from_core, first, far, out_grads, grads_core],
        after=[proj_stack],
        blocks={0: blocks_of(0, 1), 1: blocks_of(0, 1)},
    )
    got0 = to_place(product0, 1)
    product1, product2, product3 = run(
        product_kernel,
        [((rows, cols), F32)] * (line - 1),
        [here, from_core, grads, *crossed],
    )
    got1 = to_place(product1, 1)

    (partial,) = run(
        lift_kernel,
        [((rank, cols), F32)],
        [flag, product0, product1, product2, product3, projection, proj_stack, proj_others],
    )

    def halve(value, bit, exchange, after=()):
        half = value.shape[0] // 2
        mine = jnp.where(bit == 0, value[:half], value[half:])
        other = jnp.where(bit == 0, value[half:], value[:half])
        return total(mine, exchange(other), after=after)

    def double(value, bit, exchange):
        other = exchange(value)
        return jnp.where(
            bit == 0,
            jnp.concatenate([value, other]),
            jnp.concatenate([other, value]),
        )

    got2 = to_place(total(product2, got0, after=[partial]), 2)
    partial = halve(partial, core, to_core)
    inner_sum = total(inner_weights[0], to_island(inner_weights[0]), after=[partial])
    partial = halve(partial, side, to_side, after=[inner_sum])
    partial_next = to_place(partial, 1)
    grad_rows = total(product3, got1, got2, after=[partial])
    grad_other = to_island(grad_rows)
    partial = total(partial, partial_next, after=[grad_rows])
    partial_next = to_place(partial, 2)
    partial = total(partial, partial_next, after=[grad_other])
    partial = double(partial, side, to_side)
    projected = double(partial, core, to_core)

    new_first, new_second, scale = moments_and_scale(
        projected, first_moment[0, 0], second_moment[0, 0]
    )
    scale_other = to_island(scale)
    weights_block, new_momentum = run(
        outer_kernel,
        [((rows, cols // 2), BF16), ((rows, cols), F32)],
        [flag, inner_sum, grad_rows, grad_other, scale, scale_other, global_weights, outer_momentum],
    )
    return (weights_block, new_momentum, new_first[None, None], new_second[None, None])


def solution(mesh):
    placed = (
        P("island", "fsdp", None),
        P("island", "fsdp", None),
        P("fsdp", None),
        P("island", None, None, None),
        P("island", None, None, None),
        P("island", "fsdp", None),
        P("fsdp", None),
        P("fsdp", None),
    )
    lined = mesh.shape["fsdp"] == 4 * 4 and mesh.shape["island"] == 2
    return jax.shard_map(
        line_body if lined else plain_body,
        mesh=mesh,
        in_specs=placed,
        out_specs=(
            P("fsdp", "island"),
            P("fsdp", None),
            P("island", None, None, None),
            P("island", None, None, None),
        ),
        check_vma=False,
    )
```

```python
import functools

import jax
import jax.numpy as jnp
from jax import lax
from jax.experimental import pallas as pl
from jax.experimental.pallas import tpu as pltpu
from jax.sharding import PartitionSpec as P

first_decay = 0.9
second_decay = 0.999
first_fix = 1.0 - 0.9**10
second_fix = 1.0 - 0.999**10
epsilon = 1e-08
inner_rate = 1.0
outer_rate = 0.7
outer_beta = 0.9


def outer_step(stepped_sum, global_part, momentum_part, island_count):
    pseudo_grad = global_part - stepped_sum / island_count
    momentum_next = outer_beta * momentum_part + pseudo_grad
    weights_next = (global_part - outer_rate * (pseudo_grad + outer_beta * momentum_next)).astype(
        jnp.bfloat16
    )
    return (weights_next, momentum_next)


def moments_and_scale(projected, first, second):
    new_first = first_decay * first + (1.0 - first_decay) * projected
    new_second = second_decay * second + (1.0 - second_decay) * projected * projected
    adapted = new_first / first_fix / (jnp.sqrt(new_second / second_fix) + epsilon)
    scale = jnp.sqrt(jnp.mean(adapted * adapted, axis=0, keepdims=True)) / jnp.sqrt(
        jnp.mean(projected * projected, axis=0, keepdims=True) + 1e-06
    )
    return new_first, new_second, scale


def plain_body(
    activations,
    out_grads,
    projection,
    first_moment,
    second_moment,
    inner_weights,
    global_weights,
    outer_momentum,
):
    col_total = global_weights.shape[1]
    product = lax.dot_general(
        activations[0],
        out_grads[0],
        (((0,), (0,)), ((), ())),
        preferred_element_type=jnp.float32,
    )
    grad_rows = lax.psum_scatter(product, "fsdp", scatter_dimension=0, tiled=True)
    partial_sum = lax.dot_general(
        projection.astype(jnp.float32),
        grad_rows,
        (((0,), (0,)), ((), ())),
        precision=lax.Precision.HIGHEST,
        preferred_element_type=jnp.float32,
    )
    projected = lax.psum(partial_sum, "fsdp")
    new_first, new_second, scale = moments_and_scale(
        projected, first_moment[0, 0], second_moment[0, 0]
    )
    stepped = inner_weights[0] - inner_rate * grad_rows * scale
    island_count = lax.axis_size("island")
    block_cols = col_total // island_count
    block_start = lax.axis_index("island") * block_cols
    share_total = lax.psum_scatter(stepped, "island", scatter_dimension=1, tiled=True)
    global_part = lax.dynamic_slice_in_dim(global_weights, block_start, block_cols, 1)
    momentum_part = lax.dynamic_slice_in_dim(outer_momentum, block_start, block_cols, 1)
    weights_block, momentum_block = outer_step(
        share_total, global_part, momentum_part, island_count
    )
    new_momentum = lax.all_gather(momentum_block, "island", axis=1, tiled=True)
    return (weights_block, new_momentum, new_first[None, None], new_second[None, None])


VMEM_BYTES = 32 * 1024 * 1024


def whole_block(shape):
    return pl.BlockSpec(shape, lambda *_: (0,) * len(shape))


def run(kernel, out_shapes, args, after=(), scalars=None, blocks=None, scratch=()):
    blocks = blocks or {}
    lead = 0 if scalars is None else 1
    ins = lead + len(args)

    def body(*refs):
        kernel(*refs[:ins], *refs[ins + len(after) :])

    return pl.pallas_call(
        body,
        out_shape=[jax.ShapeDtypeStruct(shape, kind) for shape, kind in out_shapes],
        grid_spec=pltpu.PrefetchScalarGridSpec(
            num_scalar_prefetch=lead,
            grid=(1,),
            in_specs=[blocks.get(i, whole_block(arg.shape)) for i, arg in enumerate(args)]
            + [pl.BlockSpec(memory_space=pl.ANY)] * len(after),
            out_specs=[whole_block(shape) for shape, _ in out_shapes],
            scratch_shapes=scratch,
        ),
        compiler_params=pltpu.CompilerParams(vmem_limit_bytes=VMEM_BYTES),
        cost_estimate=pl.CostEstimate(flops=0, bytes_accessed=0, transcendentals=0),
    )(*(() if scalars is None else (scalars,)), *args, *after)


F32 = jnp.float32
BF16 = jnp.bfloat16


def turn_kernel(at, a_ref, g_ref, first, far, rest, here, cores, passed, turned):
    tokens, features = a_ref.shape[1:]
    cols = g_ref.shape[2]
    line, rows = here.shape[:2]
    for at_col in range(0, features, tokens):
        turned[at_col : at_col + tokens, :] = (
            a_ref[0, :, at_col : at_col + tokens].astype(F32).T
        )
    for at_col in range(0, cols, tokens):
        first[at_col : at_col + tokens, :] = g_ref[0, :, at_col : at_col + tokens].astype(F32)
    side, core = at[line], at[line + 1]

    def block(k, toward, which):
        start = pl.multiple_of(((at[k] * 2 + toward) * 2 + which) * rows, 8)
        return turned[pl.ds(start, rows), :]

    first[cols:, :] = block(0, 1 - side, core)
    far[...] = block(0, 1 - side, 1 - core)
    for k in range(line):
        here[k] = block(k, side, core)
        cores[k] = block(k, side, 1 - core)
        if k:
            rest[k - 1] = block(k, 1 - side, core)
            passed[k - 1] = block(k, 1 - side, 1 - core)


def pair_kernel(*refs):
    out = refs[-1]
    for i, ref in enumerate(refs[:-1]):
        out[i % 2, i // 2] = ref[...]


def stack_kernel(*refs):
    for i, ref in enumerate(refs[:-1]):
        refs[-1][i] = ref[...]


def gather_kernel(mid, odd, out):
    out[0] = odd[0]
    out[1] = mid[...]
    out[2] = odd[1]


def half_kernel(flag, value, out):
    half = out.shape[1]
    out[...] = jnp.where(
        flag[:, :half] == 0, value[:, :half].astype(F32), value[:, half:].astype(F32)
    )


def two_kernel(g_ref, crossed, out):
    tokens = g_ref.shape[1]
    cols = g_ref.shape[2]
    for at_col in range(0, cols, tokens):
        out[0, at_col : at_col + tokens, :] = g_ref[0, :, at_col : at_col + tokens].astype(F32)
    out[1] = crossed[:cols, :]


def first_product_kernel(here, core_a, crossed, far, g_ref, core_g, out, grads):
    tokens = g_ref.shape[1]
    cols = g_ref.shape[2]
    grads[:tokens, :] = g_ref[0]
    for at_col in range(0, cols, tokens):
        span = slice(at_col, at_col + tokens)
        grads[tokens : 2 * tokens, span] = core_g[0, span, :].astype(BF16)
        grads[2 * tokens : 3 * tokens, span] = crossed[span, :].astype(BF16)
        grads[3 * tokens :, span] = core_g[1, span, :].astype(BF16)
    pieces = (here[0], core_a[0], crossed[cols:, :], far[...])
    a = jnp.concatenate([piece.astype(BF16) for piece in pieces], axis=1)
    out[...] = jnp.dot(a, grads[...], preferred_element_type=F32)


def product_kernel(k, here, core_a, crossed, grads, *outs):
    for i, out in enumerate(outs):
        pieces = (here[k + i], core_a[k + i], crossed[0, i], crossed[1, i])
        a = jnp.concatenate([piece.astype(BF16) for piece in pieces], axis=1)
        out[...] = jnp.dot(a, grads[...], preferred_element_type=F32)


def sum_kernel(*refs):
    total = refs[0][...]
    for ref in refs[1:-1]:
        total = total + ref[...]
    refs[-1][...] = total


def lift_kernel(flag, p0, p1, p2, p3, own, received, others, out):
    half = others.shape[2]
    first = flag[:, :half] == 0
    low, high = own[:, :half].astype(F32), own[:, half:].astype(F32)
    mine = (received[2], received[0], received[1], jnp.where(first, low, high))
    theirs = (others[2], others[0], others[1], jnp.where(first, high, low))
    splits = []
    for product in (p0, p1, p2, p3):
        value = product[...]
        top = value.astype(BF16)
        splits.append((top, (value - top.astype(F32)).astype(BF16)))
    totals = []
    for rows in (mine, theirs):
        total = None
        for row, parts in zip(rows, splits):
            turned = row.T.astype(BF16)
            for part in parts:
                term = jnp.dot(turned, part, preferred_element_type=F32)
                total = term if total is None else total + term
        totals.append(total)
    first = flag[...] == 0
    out[:half, :] = jnp.where(first, totals[0], totals[1])
    out[half:, :] = jnp.where(first, totals[1], totals[0])


def outer_kernel(
    flag, inner_sum, grad, grad_other, scale, scale_other, weights, momentum, out, momentum_out
):
    first_island = flag[...] == 0
    own, other = grad[...] * scale[...], grad_other[...] * scale_other[...]
    first, second = jnp.where(first_island, own, other), jnp.where(first_island, other, own)
    total = (inner_sum[...] - inner_rate * first) - inner_rate * second
    weights_next, momentum_next = outer_step(total, weights[...], momentum[...], 2)
    half = out.shape[1]
    out[...] = jnp.where(
        flag[:, :half] == 0,
        weights_next[:, :half].astype(F32),
        weights_next[:, half:].astype(F32),
    ).astype(BF16)
    momentum_out[...] = momentum_next


def line_body(
    activations,
    out_grads,
    projection,
    first_moment,
    second_moment,
    inner_weights,
    global_weights,
    outer_momentum,
):
    fsdp = lax.axis_size("fsdp")
    line = fsdp // 4
    me = lax.axis_index("fsdp")
    place, side, core = me // 4, (me // 2) % 2, me % 2
    rows = projection.shape[0]
    tokens, features = activations.shape[1:]
    cols = global_weights.shape[1]
    rank = projection.shape[1]

    def move(value, target):
        pairs = []
        for f in range(fsdp):
            to = target(f // 4, (f // 2) % 2, f % 2)
            if to is not None:
                pairs.append((f, (to[0] * 2 + to[1]) * 2 + to[2]))
        return lax.ppermute(value, "fsdp", pairs)

    def to_core(value):
        return move(value, lambda l, x, c: (l, x, 1 - c))

    def to_side(value):
        return move(value, lambda l, x, c: (l, 1 - x, c))

    def to_far(value):
        return move(value, lambda l, x, c: (l, 1 - x, 1 - c))

    def to_place(value, mask):
        return move(value, lambda l, x, c: (l ^ mask, x, c))

    def to_island(value):
        return lax.ppermute(value, "island", [(0, 1), (1, 0)])

    island = lax.axis_index("island")
    at = jnp.stack([place ^ 3, place ^ 1, place ^ 2, place, side, core]).astype(jnp.int32)
    flag = jnp.full((1, cols), island, F32)

    block_shape = (rows, tokens)
    first, far, rest, here, cores, passed = run(
        turn_kernel,
        [
            ((cols + rows, tokens), F32),
            (block_shape, F32),
            ((line - 1, *block_shape), F32),
            ((line, *block_shape), F32),
            ((line, *block_shape), F32),
            ((line - 1, *block_shape), F32),
        ],
        [activations, out_grads],
        scalars=at,
        scratch=[pltpu.VMEM((features, tokens), F32)],
    )
    first = to_side(first)
    far = to_far(far)
    from_core = to_core(cores)
    passed = to_core(passed)

    def blocks_of(start, count):
        return pl.BlockSpec((count, *block_shape), lambda *_: (start // count, 0, 0))

    def cross(k, count, after):
        parts = []
        for i in range(count):
            parts += [rest[k - 1 + i], passed[k - 1 + i]]
        (paired,) = run(
            pair_kernel, [((2, count, *block_shape), F32)], parts, after=after
        )
        return to_side(paired)

    def total(*terms, after=()):
        return run(sum_kernel, [(terms[0].shape, F32)], terms, after=after)[0]

    half_rank = (rows, rank // 2)
    (proj_half,) = run(half_kernel, [(half_rank, F32)], [flag, projection])
    proj_mid = to_place(proj_half, 2)
    (proj_two,) = run(stack_kernel, [((2, *half_rank), F32)], [proj_half, proj_mid])
    proj_odd = to_place(proj_two, 1)
    (grads_two,) = run(
        two_kernel, [((2, cols, tokens), F32)], [out_grads, first], after=[far, proj_odd]
    )
    grads_core = to_core(grads_two)
    product0, grads = run(
        first_product_kernel,
        [((rows, cols), F32), ((4 * tokens, cols), BF16)],
        [here, from_core, first, far, out_grads, grads_core],
        blocks={0: blocks_of(0, 1), 1: blocks_of(0, 1)},
    )
    got0 = to_place(product0, 1)
    crossed12 = cross(1, 2, [grads_two])
    crossed3 = cross(3, 1, [product0])
    (proj_stack,) = run(
        gather_kernel, [((3, *half_rank), F32)], [proj_mid, proj_odd], after=[product0]
    )
    proj_others = to_island(proj_stack)

    def multiply(k, count, crossed, after):
        return run(
            functools.partial(product_kernel, k),
            [((rows, cols), F32)] * count,
            [here, from_core, crossed, grads],
            after=after,
        )

    inner_sum = total(inner_weights[0], to_island(inner_weights[0]), after=[proj_stack])
    product1, product2 = multiply(1, 2, crossed12, [inner_sum])
    got1 = to_place(product1, 1)
    sum2 = total(product2, got0, after=[product1])
    got2 = to_place(sum2, 2)
    (product3,) = multiply(3, 1, crossed3, [sum2])

    (partial,) = run(
        lift_kernel,
        [((rank, cols), F32)],
        [flag, product0, product1, product2, product3, projection, proj_stack, proj_others],
    )

    def double(value, bit, exchange):
        other = exchange(value)
        return jnp.where(
            bit == 0,
            jnp.concatenate([value, other]),
            jnp.concatenate([other, value]),
        )

    def halves(value, bit):
        half = value.shape[0] // 2
        low, high = value[:half], value[half:]
        return jnp.where(bit == 0, low, high), jnp.where(bit == 0, high, low)

    quarters = partial.reshape(2, 2, rank // 4, cols)
    mine = jnp.where(side == 0, quarters[:, 0], quarters[:, 1]).reshape(rank // 2, cols)
    theirs = jnp.where(side == 0, quarters[:, 1], quarters[:, 0]).reshape(rank // 2, cols)
    theirs = to_side(theirs)
    grad_rows = total(product3, got1, got2, after=[partial])
    partial = total(mine, theirs, after=[grad_rows])
    mine, theirs = halves(partial, core)
    partial = total(mine, to_core(theirs))
    partial_next = to_place(partial, 1)
    grad_other = to_island(grad_rows)
    partial = total(partial, partial_next)
    partial_next = to_place(partial, 2)
    partial = total(partial, partial_next, after=[grad_other])
    partial = double(partial, side, to_side)
    projected = double(partial, core, to_core)

    new_first, new_second, scale = moments_and_scale(
        projected, first_moment[0, 0], second_moment[0, 0]
    )
    scale_other = to_island(scale)
    weights_block, new_momentum = run(
        outer_kernel,
        [((rows, cols // 2), BF16), ((rows, cols), F32)],
        [flag, inner_sum, grad_rows, grad_other, scale, scale_other, global_weights, outer_momentum],
    )
    return (weights_block, new_momentum, new_first[None, None], new_second[None, None])


def solution(mesh):
    placed = (
        P("island", "fsdp", None),
        P("island", "fsdp", None),
        P("fsdp", None),
        P("island", None, None, None),
        P("island", None, None, None),
        P("island", "fsdp", None),
        P("fsdp", None),
        P("fsdp", None),
    )
    lined = mesh.shape["fsdp"] == 4 * 4 and mesh.shape["island"] == 2
    return jax.shard_map(
        line_body if lined else plain_body,
        mesh=mesh,
        in_specs=placed,
        out_specs=(
            P("fsdp", "island"),
            P("fsdp", None),
            P("island", None, None, None),
            P("island", None, None, None),
        ),
        check_vma=False,
    )
```

```python
import functools

import jax
import jax.numpy as jnp
from jax import lax
from jax.experimental import pallas as pl
from jax.experimental.pallas import tpu as pltpu
from jax.sharding import PartitionSpec as P

first_decay = 0.9
second_decay = 0.999
first_fix = 1.0 - 0.9**10
second_fix = 1.0 - 0.999**10
epsilon = 1e-08
inner_rate = 1.0
outer_rate = 0.7
outer_beta = 0.9


def outer_step(stepped_sum, global_part, momentum_part, island_count):
    pseudo_grad = global_part - stepped_sum / island_count
    momentum_next = outer_beta * momentum_part + pseudo_grad
    weights_next = (global_part - outer_rate * (pseudo_grad + outer_beta * momentum_next)).astype(
        jnp.bfloat16
    )
    return (weights_next, momentum_next)


def moments_and_scale(projected, first, second):
    new_first = first_decay * first + (1.0 - first_decay) * projected
    new_second = second_decay * second + (1.0 - second_decay) * projected * projected
    adapted = new_first / first_fix / (jnp.sqrt(new_second / second_fix) + epsilon)
    scale = jnp.sqrt(jnp.mean(adapted * adapted, axis=0, keepdims=True)) / jnp.sqrt(
        jnp.mean(projected * projected, axis=0, keepdims=True) + 1e-06
    )
    return new_first, new_second, scale


def plain_body(
    activations,
    out_grads,
    projection,
    first_moment,
    second_moment,
    inner_weights,
    global_weights,
    outer_momentum,
):
    col_total = global_weights.shape[1]
    product = lax.dot_general(
        activations[0],
        out_grads[0],
        (((0,), (0,)), ((), ())),
        preferred_element_type=jnp.float32,
    )
    grad_rows = lax.psum_scatter(product, "fsdp", scatter_dimension=0, tiled=True)
    partial_sum = lax.dot_general(
        projection.astype(jnp.float32),
        grad_rows,
        (((0,), (0,)), ((), ())),
        precision=lax.Precision.HIGHEST,
        preferred_element_type=jnp.float32,
    )
    projected = lax.psum(partial_sum, "fsdp")
    new_first, new_second, scale = moments_and_scale(
        projected, first_moment[0, 0], second_moment[0, 0]
    )
    stepped = inner_weights[0] - inner_rate * grad_rows * scale
    island_count = lax.axis_size("island")
    block_cols = col_total // island_count
    block_start = lax.axis_index("island") * block_cols
    share_total = lax.psum_scatter(stepped, "island", scatter_dimension=1, tiled=True)
    global_part = lax.dynamic_slice_in_dim(global_weights, block_start, block_cols, 1)
    momentum_part = lax.dynamic_slice_in_dim(outer_momentum, block_start, block_cols, 1)
    weights_block, momentum_block = outer_step(
        share_total, global_part, momentum_part, island_count
    )
    new_momentum = lax.all_gather(momentum_block, "island", axis=1, tiled=True)
    return (weights_block, new_momentum, new_first[None, None], new_second[None, None])


VMEM_BYTES = 32 * 1024 * 1024


def whole_block(shape):
    return pl.BlockSpec(shape, lambda *_: (0,) * len(shape))


def run(kernel, out_shapes, args, after=(), scalars=None, blocks=None, scratch=()):
    blocks = blocks or {}
    lead = 0 if scalars is None else 1
    ins = lead + len(args)

    def body(*refs):
        kernel(*refs[:ins], *refs[ins + len(after) :])

    return pl.pallas_call(
        body,
        out_shape=[jax.ShapeDtypeStruct(shape, kind) for shape, kind in out_shapes],
        grid_spec=pltpu.PrefetchScalarGridSpec(
            num_scalar_prefetch=lead,
            grid=(1,),
            in_specs=[blocks.get(i, whole_block(arg.shape)) for i, arg in enumerate(args)]
            + [pl.BlockSpec(memory_space=pl.ANY)] * len(after),
            out_specs=[whole_block(shape) for shape, _ in out_shapes],
            scratch_shapes=scratch,
        ),
        compiler_params=pltpu.CompilerParams(vmem_limit_bytes=VMEM_BYTES),
        cost_estimate=pl.CostEstimate(flops=0, bytes_accessed=0, transcendentals=0),
    )(*(() if scalars is None else (scalars,)), *args, *after)


F32 = jnp.float32
BF16 = jnp.bfloat16


def turn_kernel(at, a_ref, g_ref, first, far, rest, here, cores, passed, turned):
    tokens, features = a_ref.shape[1:]
    cols = g_ref.shape[2]
    line, rows = here.shape[:2]
    for at_col in range(0, features, tokens):
        turned[at_col : at_col + tokens, :] = (
            a_ref[0, :, at_col : at_col + tokens].astype(F32).T
        )
    for at_col in range(0, cols, tokens):
        first[at_col : at_col + tokens, :] = g_ref[0, :, at_col : at_col + tokens].astype(F32)
    side, core = at[line], at[line + 1]

    def block(k, toward, which):
        start = pl.multiple_of(((at[k] * 2 + toward) * 2 + which) * rows, 8)
        return turned[pl.ds(start, rows), :]

    first[cols:, :] = block(0, 1 - side, core)
    far[...] = block(0, 1 - side, 1 - core)
    for k in range(line):
        here[k] = block(k, side, core)
        cores[k] = block(k, side, 1 - core)
        if k:
            rest[k - 1] = block(k, 1 - side, core)
            passed[k - 1] = block(k, 1 - side, 1 - core)


def pair_kernel(*refs):
    out = refs[-1]
    for i, ref in enumerate(refs[:-1]):
        out[i % 2, i // 2] = ref[...]


def stack_kernel(*refs):
    for i, ref in enumerate(refs[:-1]):
        refs[-1][i] = ref[...]


def gather_kernel(mid, odd, out):
    out[0] = odd[0]
    out[1] = mid[...]
    out[2] = odd[1]


def half_kernel(flag, value, out):
    half = out.shape[1]
    out[...] = jnp.where(
        flag[:, :half] == 0, value[:, :half].astype(F32), value[:, half:].astype(F32)
    )


def two_kernel(g_ref, crossed, out):
    tokens = g_ref.shape[1]
    cols = g_ref.shape[2]
    for at_col in range(0, cols, tokens):
        out[0, at_col : at_col + tokens, :] = g_ref[0, :, at_col : at_col + tokens].astype(F32)
    out[1] = crossed[:cols, :]


def first_product_kernel(here, core_a, crossed, far, g_ref, core_g, out, grads):
    tokens = g_ref.shape[1]
    cols = g_ref.shape[2]
    grads[:tokens, :] = g_ref[0]
    for at_col in range(0, cols, tokens):
        span = slice(at_col, at_col + tokens)
        grads[tokens : 2 * tokens, span] = core_g[0, span, :].astype(BF16)
        grads[2 * tokens : 3 * tokens, span] = crossed[span, :].astype(BF16)
        grads[3 * tokens :, span] = core_g[1, span, :].astype(BF16)
    pieces = (here[0], core_a[0], crossed[cols:, :], far[...])
    a = jnp.concatenate([piece.astype(BF16) for piece in pieces], axis=1)
    out[...] = jnp.dot(a, grads[...], preferred_element_type=F32)


def product_kernel(k, here, core_a, crossed, grads, *outs):
    for i, out in enumerate(outs):
        pieces = (here[k + i], core_a[k + i], crossed[0, i], crossed[1, i])
        a = jnp.concatenate([piece.astype(BF16) for piece in pieces], axis=1)
        out[...] = jnp.dot(a, grads[...], preferred_element_type=F32)


def sum_kernel(*refs):
    total = refs[0][...]
    for ref in refs[1:-1]:
        total = total + ref[...]
    refs[-1][...] = total


def lift_kernel(flag, p0, p1, p2, p3, own, received, others, out):
    half = others.shape[2]
    first = flag[:, :half] == 0
    low, high = own[:, :half].astype(F32), own[:, half:].astype(F32)
    mine = (received[2], received[0], received[1], jnp.where(first, low, high))
    theirs = (others[2], others[0], others[1], jnp.where(first, high, low))
    splits = []
    for product in (p0, p1, p2, p3):
        value = product[...]
        top = value.astype(BF16)
        splits.append((top, (value - top.astype(F32)).astype(BF16)))
    totals = []
    for rows in (mine, theirs):
        total = None
        for row, parts in zip(rows, splits):
            turned = row.T.astype(BF16)
            for part in parts:
                term = jnp.dot(turned, part, preferred_element_type=F32)
                total = term if total is None else total + term
        totals.append(total)
    first = flag[...] == 0
    out[:half, :] = jnp.where(first, totals[0], totals[1])
    out[half:, :] = jnp.where(first, totals[1], totals[0])


def outer_kernel(
    flag, inner_sum, grad, grad_other, scale, scale_other, weights, momentum, out, momentum_out
):
    first_island = flag[...] == 0
    own, other = grad[...] * scale[...], grad_other[...] * scale_other[...]
    first, second = jnp.where(first_island, own, other), jnp.where(first_island, other, own)
    total = (inner_sum[...] - inner_rate * first) - inner_rate * second
    weights_next, momentum_next = outer_step(total, weights[...], momentum[...], 2)
    half = out.shape[1]
    out[...] = jnp.where(
        flag[:, :half] == 0,
        weights_next[:, :half].astype(F32),
        weights_next[:, half:].astype(F32),
    ).astype(BF16)
    momentum_out[...] = momentum_next


def line_body(
    activations,
    out_grads,
    projection,
    first_moment,
    second_moment,
    inner_weights,
    global_weights,
    outer_momentum,
):
    fsdp = lax.axis_size("fsdp")
    line = fsdp // 4
    me = lax.axis_index("fsdp")
    place, side, core = me // 4, (me // 2) % 2, me % 2
    rows = projection.shape[0]
    tokens, features = activations.shape[1:]
    cols = global_weights.shape[1]
    rank = projection.shape[1]

    def move(value, target):
        pairs = []
        for f in range(fsdp):
            to = target(f // 4, (f // 2) % 2, f % 2)
            if to is not None:
                pairs.append((f, (to[0] * 2 + to[1]) * 2 + to[2]))
        return lax.ppermute(value, "fsdp", pairs)

    def to_core(value):
        return move(value, lambda l, x, c: (l, x, 1 - c))

    def to_side(value):
        return move(value, lambda l, x, c: (l, 1 - x, c))

    def to_far(value):
        return move(value, lambda l, x, c: (l, 1 - x, 1 - c))

    def to_place(value, mask):
        return move(value, lambda l, x, c: (l ^ mask, x, c))

    def to_island(value):
        return lax.ppermute(value, "island", [(0, 1), (1, 0)])

    island = lax.axis_index("island")
    at = jnp.stack([place ^ 3, place ^ 1, place ^ 2, place, side, core]).astype(jnp.int32)
    flag = jnp.full((1, cols), island, F32)

    block_shape = (rows, tokens)
    first, far, rest, here, cores, passed = run(
        turn_kernel,
        [
            ((cols + rows, tokens), F32),
            (block_shape, F32),
            ((line - 1, *block_shape), F32),
            ((line, *block_shape), F32),
            ((line, *block_shape), F32),
            ((line - 1, *block_shape), F32),
        ],
        [activations, out_grads],
        scalars=at,
        scratch=[pltpu.VMEM((features, tokens), F32)],
    )
    first = to_side(first)
    far = to_far(far)
    from_core = to_core(cores)
    passed = to_core(passed)

    def blocks_of(start, count):
        return pl.BlockSpec((count, *block_shape), lambda *_: (start // count, 0, 0))

    def cross(k, count, after):
        parts = []
        for i in range(count):
            parts += [rest[k - 1 + i], passed[k - 1 + i]]
        (paired,) = run(
            pair_kernel, [((2, count, *block_shape), F32)], parts, after=after
        )
        return to_side(paired)

    def total(*terms, after=()):
        return run(sum_kernel, [(terms[0].shape, F32)], terms, after=after)[0]

    half_rank = (rows, rank // 2)
    (proj_half,) = run(half_kernel, [(half_rank, F32)], [flag, projection])
    proj_mid = to_place(proj_half, 2)
    (proj_two,) = run(stack_kernel, [((2, *half_rank), F32)], [proj_half, proj_mid])
    proj_odd = to_place(proj_two, 1)
    (grads_two,) = run(
        two_kernel, [((2, cols, tokens), F32)], [out_grads, first], after=[far, proj_odd]
    )
    grads_core = to_core(grads_two)
    product0, grads = run(
        first_product_kernel,
        [((rows, cols), F32), ((4 * tokens, cols), BF16)],
        [here, from_core, first, far, out_grads, grads_core],
        blocks={0: blocks_of(0, 1), 1: blocks_of(0, 1)},
    )
    got0 = to_place(product0, 1)
    crossed12 = cross(1, 2, [grads_two])
    crossed3 = cross(3, 1, [product0])
    (proj_stack,) = run(
        gather_kernel, [((3, *half_rank), F32)], [proj_mid, proj_odd], after=[product0]
    )
    proj_others = to_island(proj_stack)

    def multiply(k, count, crossed, after):
        return run(
            functools.partial(product_kernel, k),
            [((rows, cols), F32)] * count,
            [here, from_core, crossed, grads],
            after=after,
        )

    product1, product2 = multiply(1, 2, crossed12, [proj_stack])
    got1 = to_place(product1, 1)
    sum2 = total(product2, got0, after=[product1])
    got2 = to_place(sum2, 2)
    inner_sum = total(inner_weights[0], to_island(inner_weights[0]), after=[sum2])
    (product3,) = multiply(3, 1, crossed3, [inner_sum])

    (partial,) = run(
        lift_kernel,
        [((rank, cols), F32)],
        [flag, product0, product1, product2, product3, projection, proj_stack, proj_others],
    )

    def double(value, bit, exchange):
        other = exchange(value)
        return jnp.where(
            bit == 0,
            jnp.concatenate([value, other]),
            jnp.concatenate([other, value]),
        )

    def halves(value, bit):
        half = value.shape[0] // 2
        low, high = value[:half], value[half:]
        return jnp.where(bit == 0, low, high), jnp.where(bit == 0, high, low)

    quarter_rows = rank // 4
    number = 2 * core + side

    def quarter_of(which):
        return lax.select_n(
            which,
            *(partial[q * quarter_rows : (q + 1) * quarter_rows] for q in range(4)),
        )

    terms = [
        quarter_of(number),
        to_far(quarter_of(number ^ 3)),
        to_side(quarter_of(number ^ 1)),
        to_core(quarter_of(number ^ 2)),
    ]
    grad_rows = total(product3, got1, got2, after=[partial])
    partial = total(*terms, after=[got1, got2])
    partial_next = to_place(partial, 1)
    grad_other = to_island(grad_rows)
    partial = total(partial, partial_next)
    partial_next = to_place(partial, 2)
    partial = total(partial, partial_next)
    partial = total(double(partial, side, to_side), after=[grad_other])
    projected = double(partial, core, to_core)

    new_first, new_second, scale = moments_and_scale(
        projected, first_moment[0, 0], second_moment[0, 0]
    )
    scale_other = to_island(scale)
    weights_block, new_momentum = run(
        outer_kernel,
        [((rows, cols // 2), BF16), ((rows, cols), F32)],
        [flag, inner_sum, grad_rows, grad_other, scale, scale_other, global_weights, outer_momentum],
    )
    return (weights_block, new_momentum, new_first[None, None], new_second[None, None])


def solution(mesh):
    placed = (
        P("island", "fsdp", None),
        P("island", "fsdp", None),
        P("fsdp", None),
        P("island", None, None, None),
        P("island", None, None, None),
        P("island", "fsdp", None),
        P("fsdp", None),
        P("fsdp", None),
    )
    lined = mesh.shape["fsdp"] == 4 * 4 and mesh.shape["island"] == 2
    return jax.shard_map(
        line_body if lined else plain_body,
        mesh=mesh,
        in_specs=placed,
        out_specs=(
            P("fsdp", "island"),
            P("fsdp", None),
            P("island", None, None, None),
            P("island", None, None, None),
        ),
        check_vma=False,
    )
```

```python
import functools

import jax
import jax.numpy as jnp
from jax import lax
from jax.experimental import pallas as pl
from jax.experimental.pallas import tpu as pltpu
from jax.sharding import PartitionSpec as P

first_decay = 0.9
second_decay = 0.999
first_fix = 1.0 - 0.9**10
second_fix = 1.0 - 0.999**10
epsilon = 1e-08
inner_rate = 1.0
outer_rate = 0.7
outer_beta = 0.9


def outer_step(stepped_sum, global_part, momentum_part, island_count):
    pseudo_grad = global_part - stepped_sum / island_count
    momentum_next = outer_beta * momentum_part + pseudo_grad
    weights_next = (global_part - outer_rate * (pseudo_grad + outer_beta * momentum_next)).astype(
        jnp.bfloat16
    )
    return (weights_next, momentum_next)


def moments_and_scale(projected, first, second):
    new_first = first_decay * first + (1.0 - first_decay) * projected
    new_second = second_decay * second + (1.0 - second_decay) * projected * projected
    adapted = new_first / first_fix / (jnp.sqrt(new_second / second_fix) + epsilon)
    scale = jnp.sqrt(jnp.mean(adapted * adapted, axis=0, keepdims=True)) / jnp.sqrt(
        jnp.mean(projected * projected, axis=0, keepdims=True) + 1e-06
    )
    return new_first, new_second, scale


def plain_body(
    activations,
    out_grads,
    projection,
    first_moment,
    second_moment,
    inner_weights,
    global_weights,
    outer_momentum,
):
    col_total = global_weights.shape[1]
    product = lax.dot_general(
        activations[0],
        out_grads[0],
        (((0,), (0,)), ((), ())),
        preferred_element_type=jnp.float32,
    )
    grad_rows = lax.psum_scatter(product, "fsdp", scatter_dimension=0, tiled=True)
    partial_sum = lax.dot_general(
        projection.astype(jnp.float32),
        grad_rows,
        (((0,), (0,)), ((), ())),
        precision=lax.Precision.HIGHEST,
        preferred_element_type=jnp.float32,
    )
    projected = lax.psum(partial_sum, "fsdp")
    new_first, new_second, scale = moments_and_scale(
        projected, first_moment[0, 0], second_moment[0, 0]
    )
    stepped = inner_weights[0] - inner_rate * grad_rows * scale
    island_count = lax.axis_size("island")
    block_cols = col_total // island_count
    block_start = lax.axis_index("island") * block_cols
    share_total = lax.psum_scatter(stepped, "island", scatter_dimension=1, tiled=True)
    global_part = lax.dynamic_slice_in_dim(global_weights, block_start, block_cols, 1)
    momentum_part = lax.dynamic_slice_in_dim(outer_momentum, block_start, block_cols, 1)
    weights_block, momentum_block = outer_step(
        share_total, global_part, momentum_part, island_count
    )
    new_momentum = lax.all_gather(momentum_block, "island", axis=1, tiled=True)
    return (weights_block, new_momentum, new_first[None, None], new_second[None, None])


VMEM_BYTES = 32 * 1024 * 1024


def whole_block(shape):
    return pl.BlockSpec(shape, lambda *_: (0,) * len(shape))


def run(kernel, out_shapes, args, after=(), scalars=None, blocks=None, scratch=()):
    blocks = blocks or {}
    lead = 0 if scalars is None else 1
    ins = lead + len(args)

    def body(*refs):
        kernel(*refs[:ins], *refs[ins + len(after) :])

    return pl.pallas_call(
        body,
        out_shape=[jax.ShapeDtypeStruct(shape, kind) for shape, kind in out_shapes],
        grid_spec=pltpu.PrefetchScalarGridSpec(
            num_scalar_prefetch=lead,
            grid=(1,),
            in_specs=[blocks.get(i, whole_block(arg.shape)) for i, arg in enumerate(args)]
            + [pl.BlockSpec(memory_space=pl.ANY)] * len(after),
            out_specs=[whole_block(shape) for shape, _ in out_shapes],
            scratch_shapes=scratch,
        ),
        compiler_params=pltpu.CompilerParams(vmem_limit_bytes=VMEM_BYTES),
        cost_estimate=pl.CostEstimate(flops=0, bytes_accessed=0, transcendentals=0),
    )(*(() if scalars is None else (scalars,)), *args, *after)


F32 = jnp.float32
BF16 = jnp.bfloat16


def turn_kernel(at, a_ref, g_ref, first, far, rest, here, cores, passed, turned):
    tokens, features = a_ref.shape[1:]
    cols = g_ref.shape[2]
    line, rows = here.shape[:2]
    for at_col in range(0, features, tokens):
        turned[at_col : at_col + tokens, :] = (
            a_ref[0, :, at_col : at_col + tokens].astype(F32).T
        )
    for at_col in range(0, cols, tokens):
        first[at_col : at_col + tokens, :] = g_ref[0, :, at_col : at_col + tokens].astype(F32)
    side, core = at[line], at[line + 1]

    def block(k, toward, which):
        start = pl.multiple_of(((at[k] * 2 + toward) * 2 + which) * rows, 8)
        return turned[pl.ds(start, rows), :]

    first[cols:, :] = block(0, 1 - side, core)
    far[...] = block(0, 1 - side, 1 - core)
    for k in range(line):
        here[k] = block(k, side, core)
        cores[k] = block(k, side, 1 - core)
        if k:
            rest[k - 1] = block(k, 1 - side, core)
            passed[k - 1] = block(k, 1 - side, 1 - core)


def pair_kernel(*refs):
    out = refs[-1]
    for i, ref in enumerate(refs[:-1]):
        out[i % 2, i // 2] = ref[...]


def stack_kernel(*refs):
    for i, ref in enumerate(refs[:-1]):
        refs[-1][i] = ref[...]


def gather_kernel(mid, odd, out):
    out[0] = odd[0]
    out[1] = mid[...]
    out[2] = odd[1]


def half_kernel(flag, value, out):
    half = out.shape[1]
    out[...] = jnp.where(
        flag[:, :half] == 0, value[:, :half].astype(F32), value[:, half:].astype(F32)
    )


def two_kernel(g_ref, crossed, out):
    tokens = g_ref.shape[1]
    cols = g_ref.shape[2]
    for at_col in range(0, cols, tokens):
        out[0, at_col : at_col + tokens, :] = g_ref[0, :, at_col : at_col + tokens].astype(F32)
    out[1] = crossed[:cols, :]


def first_product_kernel(here, core_a, crossed, far, g_ref, core_g, out, grads):
    tokens = g_ref.shape[1]
    cols = g_ref.shape[2]
    grads[:tokens, :] = g_ref[0]
    for at_col in range(0, cols, tokens):
        span = slice(at_col, at_col + tokens)
        grads[tokens : 2 * tokens, span] = core_g[0, span, :].astype(BF16)
        grads[2 * tokens : 3 * tokens, span] = crossed[span, :].astype(BF16)
        grads[3 * tokens :, span] = core_g[1, span, :].astype(BF16)
    pieces = (here[0], core_a[0], crossed[cols:, :], far[...])
    a = jnp.concatenate([piece.astype(BF16) for piece in pieces], axis=1)
    out[...] = jnp.dot(a, grads[...], preferred_element_type=F32)


def later_product(k, i, here, core_a, crossed, grads):
    pieces = (here[k], core_a[k], crossed[0, i], crossed[1, i])
    a = jnp.concatenate([piece.astype(BF16) for piece in pieces], axis=1)
    return jnp.dot(a, grads[...], preferred_element_type=F32)


def product_kernel(k, i, here, core_a, crossed, grads, out):
    out[...] = later_product(k, i, here, core_a, crossed, grads)


def product_and_sum_kernel(here, core_a, crossed, grads, got, out, out_sum):
    product = later_product(2, 1, here, core_a, crossed, grads)
    out[...] = product
    out_sum[...] = product + got[...]


def sum_kernel(*refs):
    total = refs[0][...]
    for ref in refs[1:-1]:
        total = total + ref[...]
    refs[-1][...] = total


def lift_kernel(flag, p0, p1, p2, p3, own, received, others, out):
    half = others.shape[2]
    first = flag[:, :half] == 0
    low, high = own[:, :half].astype(F32), own[:, half:].astype(F32)
    mine = (received[2], received[0], received[1], jnp.where(first, low, high))
    theirs = (others[2], others[0], others[1], jnp.where(first, high, low))
    splits = []
    for product in (p0, p1, p2, p3):
        value = product[...]
        top = value.astype(BF16)
        splits.append((top, (value - top.astype(F32)).astype(BF16)))
    totals = []
    for rows in (mine, theirs):
        total = None
        for row, parts in zip(rows, splits):
            turned = row.T.astype(BF16)
            for part in parts:
                term = jnp.dot(turned, part, preferred_element_type=F32)
                total = term if total is None else total + term
        totals.append(total)
    first = flag[...] == 0
    out[:half, :] = jnp.where(first, totals[0], totals[1])
    out[half:, :] = jnp.where(first, totals[1], totals[0])


def outer_kernel(
    flag, inner_sum, grad, grad_other, scale, scale_other, weights, momentum, out, momentum_out
):
    first_island = flag[...] == 0
    own, other = grad[...] * scale[...], grad_other[...] * scale_other[...]
    first, second = jnp.where(first_island, own, other), jnp.where(first_island, other, own)
    total = (inner_sum[...] - inner_rate * first) - inner_rate * second
    weights_next, momentum_next = outer_step(total, weights[...], momentum[...], 2)
    half = out.shape[1]
    out[...] = jnp.where(
        flag[:, :half] == 0,
        weights_next[:, :half].astype(F32),
        weights_next[:, half:].astype(F32),
    ).astype(BF16)
    momentum_out[...] = momentum_next


def line_body(
    activations,
    out_grads,
    projection,
    first_moment,
    second_moment,
    inner_weights,
    global_weights,
    outer_momentum,
):
    fsdp = lax.axis_size("fsdp")
    line = fsdp // 4
    me = lax.axis_index("fsdp")
    place, side, core = me // 4, (me // 2) % 2, me % 2
    rows = projection.shape[0]
    tokens, features = activations.shape[1:]
    cols = global_weights.shape[1]
    rank = projection.shape[1]

    def move(value, target):
        pairs = []
        for f in range(fsdp):
            to = target(f // 4, (f // 2) % 2, f % 2)
            if to is not None:
                pairs.append((f, (to[0] * 2 + to[1]) * 2 + to[2]))
        return lax.ppermute(value, "fsdp", pairs)

    def to_core(value):
        return move(value, lambda l, x, c: (l, x, 1 - c))

    def to_side(value):
        return move(value, lambda l, x, c: (l, 1 - x, c))

    def to_far(value):
        return move(value, lambda l, x, c: (l, 1 - x, 1 - c))

    def to_place(value, mask):
        return move(value, lambda l, x, c: (l ^ mask, x, c))

    def to_island(value):
        return lax.ppermute(value, "island", [(0, 1), (1, 0)])

    island = lax.axis_index("island")
    at = jnp.stack([place ^ 3, place ^ 1, place ^ 2, place, side, core]).astype(jnp.int32)
    flag = jnp.full((1, cols), island, F32)

    block_shape = (rows, tokens)
    first, far, rest, here, cores, passed = run(
        turn_kernel,
        [
            ((cols + rows, tokens), F32),
            (block_shape, F32),
            ((line - 1, *block_shape), F32),
            ((line, *block_shape), F32),
            ((line, *block_shape), F32),
            ((line - 1, *block_shape), F32),
        ],
        [activations, out_grads],
        scalars=at,
        scratch=[pltpu.VMEM((features, tokens), F32)],
    )
    first = to_side(first)
    far = to_far(far)
    from_core = to_core(cores)
    passed = to_core(passed)

    def blocks_of(start, count):
        return pl.BlockSpec((count, *block_shape), lambda *_: (start // count, 0, 0))

    def cross(k, count, after):
        parts = []
        for i in range(count):
            parts += [rest[k - 1 + i], passed[k - 1 + i]]
        (paired,) = run(
            pair_kernel, [((2, count, *block_shape), F32)], parts, after=after
        )
        return to_side(paired)

    def total(*terms, after=()):
        return run(sum_kernel, [(terms[0].shape, F32)], terms, after=after)[0]

    half_rank = (rows, rank // 2)
    (proj_half,) = run(half_kernel, [(half_rank, F32)], [flag, projection])
    proj_mid = to_place(proj_half, 2)
    (proj_two,) = run(stack_kernel, [((2, *half_rank), F32)], [proj_half, proj_mid])
    proj_odd = to_place(proj_two, 1)
    (grads_two,) = run(
        two_kernel, [((2, cols, tokens), F32)], [out_grads, first], after=[far, proj_odd]
    )
    grads_core = to_core(grads_two)
    product0, grads = run(
        first_product_kernel,
        [((rows, cols), F32), ((4 * tokens, cols), BF16)],
        [here, from_core, first, far, out_grads, grads_core],
        blocks={0: blocks_of(0, 1), 1: blocks_of(0, 1)},
    )
    got0 = to_place(product0, 1)
    crossed12 = cross(1, 2, [grads_two])
    crossed3 = cross(3, 1, [product0])
    (proj_stack,) = run(
        gather_kernel, [((3, *half_rank), F32)], [proj_mid, proj_odd], after=[product0]
    )
    proj_others = to_island(proj_stack)

    row_block = ((rows, cols), F32)
    (product1,) = run(
        functools.partial(product_kernel, 1, 0),
        [row_block],
        [here, from_core, crossed12, grads],
        after=[proj_stack],
    )
    got1 = to_place(product1, 1)
    product2, sum2 = run(
        product_and_sum_kernel,
        [row_block, row_block],
        [here, from_core, crossed12, grads, got0],
        after=[product1],
    )
    got2 = to_place(sum2, 2)
    inner_sum = total(inner_weights[0], to_island(inner_weights[0]), after=[sum2])
    (product3,) = run(
        functools.partial(product_kernel, 3, 0),
        [row_block],
        [here, from_core, crossed3, grads],
        after=[inner_sum],
    )

    (partial,) = run(
        lift_kernel,
        [((rank, cols), F32)],
        [flag, product0, product1, product2, product3, projection, proj_stack, proj_others],
    )

    def double(value, bit, exchange):
        other = exchange(value)
        return jnp.where(
            bit == 0,
            jnp.concatenate([value, other]),
            jnp.concatenate([other, value]),
        )

    def halves(value, bit):
        half = value.shape[0] // 2
        low, high = value[:half], value[half:]
        return jnp.where(bit == 0, low, high), jnp.where(bit == 0, high, low)

    quarter_rows = rank // 4
    number = 2 * core + side

    def quarter_of(which):
        return lax.select_n(
            which,
            *(partial[q * quarter_rows : (q + 1) * quarter_rows] for q in range(4)),
        )

    terms = [
        quarter_of(number),
        to_far(quarter_of(number ^ 3)),
        to_side(quarter_of(number ^ 1)),
        to_core(quarter_of(number ^ 2)),
    ]
    partial = total(*terms)
    partial_next = to_place(partial, 1)
    grad_rows = total(product3, got1, got2, after=[partial])
    grad_other = to_island(grad_rows)
    partial = total(partial, partial_next, after=[got1, got2])
    partial_next = to_place(partial, 2)
    partial = total(partial, partial_next)
    partial = double(partial, side, to_side)
    token = to_core(grad_other[: rank // 4])
    projected = total(double(partial, core, to_core), after=[token])

    new_first, new_second, scale = moments_and_scale(
        projected, first_moment[0, 0], second_moment[0, 0]
    )
    scale_other = to_island(scale)
    weights_block, new_momentum = run(
        outer_kernel,
        [((rows, cols // 2), BF16), ((rows, cols), F32)],
        [flag, inner_sum, grad_rows, grad_other, scale, scale_other, global_weights, outer_momentum],
    )
    return (weights_block, new_momentum, new_first[None, None], new_second[None, None])


def solution(mesh):
    placed = (
        P("island", "fsdp", None),
        P("island", "fsdp", None),
        P("fsdp", None),
        P("island", None, None, None),
        P("island", None, None, None),
        P("island", "fsdp", None),
        P("fsdp", None),
        P("fsdp", None),
    )
    lined = mesh.shape["fsdp"] == 4 * 4 and mesh.shape["island"] == 2
    return jax.shard_map(
        line_body if lined else plain_body,
        mesh=mesh,
        in_specs=placed,
        out_specs=(
            P("fsdp", "island"),
            P("fsdp", None),
            P("island", None, None, None),
            P("island", None, None, None),
        ),
        check_vma=False,
    )
```

```python
import functools

import jax
import jax.numpy as jnp
from jax import lax
from jax.experimental import pallas as pl
from jax.experimental.pallas import tpu as pltpu
from jax.sharding import PartitionSpec as P

first_decay = 0.9
second_decay = 0.999
first_fix = 1.0 - 0.9**10
second_fix = 1.0 - 0.999**10
epsilon = 1e-08
inner_rate = 1.0
outer_rate = 0.7
outer_beta = 0.9


def outer_step(stepped_sum, global_part, momentum_part, island_count):
    pseudo_grad = global_part - stepped_sum / island_count
    momentum_next = outer_beta * momentum_part + pseudo_grad
    weights_next = (global_part - outer_rate * (pseudo_grad + outer_beta * momentum_next)).astype(
        jnp.bfloat16
    )
    return (weights_next, momentum_next)


def moments_and_scale(projected, first, second):
    new_first = first_decay * first + (1.0 - first_decay) * projected
    new_second = second_decay * second + (1.0 - second_decay) * projected * projected
    adapted = new_first / first_fix / (jnp.sqrt(new_second / second_fix) + epsilon)
    scale = jnp.sqrt(jnp.mean(adapted * adapted, axis=0, keepdims=True)) / jnp.sqrt(
        jnp.mean(projected * projected, axis=0, keepdims=True) + 1e-06
    )
    return new_first, new_second, scale


def plain_body(
    activations,
    out_grads,
    projection,
    first_moment,
    second_moment,
    inner_weights,
    global_weights,
    outer_momentum,
):
    col_total = global_weights.shape[1]
    product = lax.dot_general(
        activations[0],
        out_grads[0],
        (((0,), (0,)), ((), ())),
        preferred_element_type=jnp.float32,
    )
    grad_rows = lax.psum_scatter(product, "fsdp", scatter_dimension=0, tiled=True)
    partial_sum = lax.dot_general(
        projection.astype(jnp.float32),
        grad_rows,
        (((0,), (0,)), ((), ())),
        precision=lax.Precision.HIGHEST,
        preferred_element_type=jnp.float32,
    )
    projected = lax.psum(partial_sum, "fsdp")
    new_first, new_second, scale = moments_and_scale(
        projected, first_moment[0, 0], second_moment[0, 0]
    )
    stepped = inner_weights[0] - inner_rate * grad_rows * scale
    island_count = lax.axis_size("island")
    block_cols = col_total // island_count
    block_start = lax.axis_index("island") * block_cols
    share_total = lax.psum_scatter(stepped, "island", scatter_dimension=1, tiled=True)
    global_part = lax.dynamic_slice_in_dim(global_weights, block_start, block_cols, 1)
    momentum_part = lax.dynamic_slice_in_dim(outer_momentum, block_start, block_cols, 1)
    weights_block, momentum_block = outer_step(
        share_total, global_part, momentum_part, island_count
    )
    new_momentum = lax.all_gather(momentum_block, "island", axis=1, tiled=True)
    return (weights_block, new_momentum, new_first[None, None], new_second[None, None])


VMEM_BYTES = 16 * 1024 * 1024


def whole_block(shape):
    return pl.BlockSpec(shape, lambda *_: (0,) * len(shape))


def run(kernel, out_shapes, args, after=(), scalars=None, blocks=None, scratch=()):
    blocks = blocks or {}
    lead = 0 if scalars is None else 1
    ins = lead + len(args)

    def body(*refs):
        kernel(*refs[:ins], *refs[ins + len(after) :])

    return pl.pallas_call(
        body,
        out_shape=[jax.ShapeDtypeStruct(shape, kind) for shape, kind in out_shapes],
        grid_spec=pltpu.PrefetchScalarGridSpec(
            num_scalar_prefetch=lead,
            grid=(1,),
            in_specs=[blocks.get(i, whole_block(arg.shape)) for i, arg in enumerate(args)]
            + [pl.BlockSpec(memory_space=pl.ANY)] * len(after),
            out_specs=[whole_block(shape) for shape, _ in out_shapes],
            scratch_shapes=scratch,
        ),
        compiler_params=pltpu.CompilerParams(vmem_limit_bytes=VMEM_BYTES),
        cost_estimate=pl.CostEstimate(flops=0, bytes_accessed=0, transcendentals=0),
    )(*(() if scalars is None else (scalars,)), *args, *after)


F32 = jnp.float32
BF16 = jnp.bfloat16


def turn_kernel(at, a_ref, g_ref, first, far, rest, here, cores, passed, turned):
    tokens, features = a_ref.shape[1:]
    cols = g_ref.shape[2]
    line, rows = here.shape[:2]
    for at_col in range(0, features, tokens):
        turned[at_col : at_col + tokens, :] = (
            a_ref[0, :, at_col : at_col + tokens].astype(F32).T
        )
    for at_col in range(0, cols, tokens):
        first[at_col : at_col + tokens, :] = g_ref[0, :, at_col : at_col + tokens].astype(F32)
    side, core = at[line], at[line + 1]

    def block(k, toward, which):
        start = pl.multiple_of(((at[k] * 2 + toward) * 2 + which) * rows, 8)
        return turned[pl.ds(start, rows), :]

    first[cols:, :] = block(0, 1 - side, core)
    far[...] = block(0, 1 - side, 1 - core)
    for k in range(line):
        here[k] = block(k, side, core)
        cores[k] = block(k, side, 1 - core)
        if k:
            rest[k - 1] = block(k, 1 - side, core)
            passed[k - 1] = block(k, 1 - side, 1 - core)


def pair_kernel(*refs):
    out = refs[-1]
    for i, ref in enumerate(refs[:-1]):
        out[i % 2, i // 2] = ref[...]


def stack_kernel(*refs):
    for i, ref in enumerate(refs[:-1]):
        refs[-1][i] = ref[...]


def gather_kernel(mid, odd, out):
    out[0] = odd[0]
    out[1] = mid[...]
    out[2] = odd[1]


def half_kernel(flag, value, out):
    half = out.shape[1]
    out[...] = jnp.where(
        flag[:, :half] == 0, value[:, :half].astype(F32), value[:, half:].astype(F32)
    )


def two_kernel(g_ref, crossed, out):
    tokens = g_ref.shape[1]
    cols = g_ref.shape[2]
    for at_col in range(0, cols, tokens):
        out[0, at_col : at_col + tokens, :] = g_ref[0, :, at_col : at_col + tokens].astype(F32)
    out[1] = crossed[:cols, :]


def first_product_kernel(here, core_a, crossed, far, g_ref, core_g, out, grads):
    tokens = g_ref.shape[1]
    cols = g_ref.shape[2]
    grads[:tokens, :] = g_ref[0]
    for at_col in range(0, cols, tokens):
        span = slice(at_col, at_col + tokens)
        grads[tokens : 2 * tokens, span] = core_g[0, span, :].astype(BF16)
        grads[2 * tokens : 3 * tokens, span] = crossed[span, :].astype(BF16)
        grads[3 * tokens :, span] = core_g[1, span, :].astype(BF16)
    pieces = (here[0], core_a[0], crossed[cols:, :], far[...])
    a = jnp.concatenate([piece.astype(BF16) for piece in pieces], axis=1)
    out[...] = jnp.dot(a, grads[...], preferred_element_type=F32)


def later_product(k, i, here, core_a, crossed, grads):
    pieces = (here[k], core_a[k], crossed[0, i], crossed[1, i])
    a = jnp.concatenate([piece.astype(BF16) for piece in pieces], axis=1)
    return jnp.dot(a, grads[...], preferred_element_type=F32)


def product_kernel(k, i, here, core_a, crossed, grads, out):
    out[...] = later_product(k, i, here, core_a, crossed, grads)


def product_and_sum_kernel(here, core_a, crossed, grads, got, out, out_sum):
    product = later_product(2, 1, here, core_a, crossed, grads)
    out[...] = product
    out_sum[...] = product + got[...]


def sum_kernel(*refs):
    total = refs[0][...]
    for ref in refs[1:-1]:
        total = total + ref[...]
    refs[-1][...] = total


def lift_kernel(flag, p0, p1, p2, p3, own, received, others, out):
    half = others.shape[2]
    first = flag[:, :half] == 0
    low, high = own[:, :half].astype(F32), own[:, half:].astype(F32)
    mine = (received[2], received[0], received[1], jnp.where(first, low, high))
    theirs = (others[2], others[0], others[1], jnp.where(first, high, low))
    splits = []
    for product in (p0, p1, p2, p3):
        value = product[...]
        top = value.astype(BF16)
        splits.append((top, (value - top.astype(F32)).astype(BF16)))
    totals = []
    for rows in (mine, theirs):
        total = None
        for row, parts in zip(rows, splits):
            turned = row.T.astype(BF16)
            for part in parts:
                term = jnp.dot(turned, part, preferred_element_type=F32)
                total = term if total is None else total + term
        totals.append(total)
    first = flag[...] == 0
    out[:half, :] = jnp.where(first, totals[0], totals[1])
    out[half:, :] = jnp.where(first, totals[1], totals[0])


def scale_kernel(projected, first, second, out):
    _, _, out[...] = moments_and_scale(projected[...], first[...], second[...])


def outer_kernel(
    flag, inner_sum, grad, grad_other, scale, scale_other, weights, momentum, out, momentum_out
):
    first_island = flag[...] == 0
    own, other = grad[...] * scale[...], grad_other[...] * scale_other[...]
    first, second = jnp.where(first_island, own, other), jnp.where(first_island, other, own)
    total = (inner_sum[...] - inner_rate * first) - inner_rate * second
    weights_next, momentum_next = outer_step(total, weights[...], momentum[...], 2)
    half = out.shape[1]
    out[...] = jnp.where(
        flag[:, :half] == 0,
        weights_next[:, :half].astype(F32),
        weights_next[:, half:].astype(F32),
    ).astype(BF16)
    momentum_out[...] = momentum_next


def line_body(
    activations,
    out_grads,
    projection,
    first_moment,
    second_moment,
    inner_weights,
    global_weights,
    outer_momentum,
):
    fsdp = lax.axis_size("fsdp")
    line = fsdp // 4
    me = lax.axis_index("fsdp")
    place, side, core = me // 4, (me // 2) % 2, me % 2
    rows = projection.shape[0]
    tokens, features = activations.shape[1:]
    cols = global_weights.shape[1]
    rank = projection.shape[1]

    def move(value, target):
        pairs = []
        for f in range(fsdp):
            to = target(f // 4, (f // 2) % 2, f % 2)
            if to is not None:
                pairs.append((f, (to[0] * 2 + to[1]) * 2 + to[2]))
        return lax.ppermute(value, "fsdp", pairs)

    def to_core(value):
        return move(value, lambda l, x, c: (l, x, 1 - c))

    def to_side(value):
        return move(value, lambda l, x, c: (l, 1 - x, c))

    def to_far(value):
        return move(value, lambda l, x, c: (l, 1 - x, 1 - c))

    def to_place(value, mask):
        return move(value, lambda l, x, c: (l ^ mask, x, c))

    def to_island(value):
        return lax.ppermute(value, "island", [(0, 1), (1, 0)])

    island = lax.axis_index("island")
    at = jnp.stack([place ^ 3, place ^ 1, place ^ 2, place, side, core]).astype(jnp.int32)
    flag = jnp.full((1, cols), island, F32)

    block_shape = (rows, tokens)
    first, far, rest, here, cores, passed = run(
        turn_kernel,
        [
            ((cols + rows, tokens), F32),
            (block_shape, F32),
            ((line - 1, *block_shape), F32),
            ((line, *block_shape), F32),
            ((line, *block_shape), F32),
            ((line - 1, *block_shape), F32),
        ],
        [activations, out_grads],
        scalars=at,
        scratch=[pltpu.VMEM((features, tokens), F32)],
    )
    first = to_side(first)
    far = to_far(far)
    from_core = to_core(cores)
    passed = to_core(passed)

    def blocks_of(start, count):
        return pl.BlockSpec((count, *block_shape), lambda *_: (start // count, 0, 0))

    def cross(k, count, after):
        parts = []
        for i in range(count):
            parts += [rest[k - 1 + i], passed[k - 1 + i]]
        (paired,) = run(
            pair_kernel, [((2, count, *block_shape), F32)], parts, after=after
        )
        return to_side(paired)

    def total(*terms, after=()):
        return run(sum_kernel, [(terms[0].shape, F32)], terms, after=after)[0]

    half_rank = (rows, rank // 2)
    (proj_half,) = run(half_kernel, [(half_rank, F32)], [flag, projection])
    proj_mid = to_place(proj_half, 2)
    (proj_two,) = run(stack_kernel, [((2, *half_rank), F32)], [proj_half, proj_mid])
    proj_odd = to_place(proj_two, 1)
    (grads_two,) = run(
        two_kernel, [((2, cols, tokens), F32)], [out_grads, first], after=[far, proj_odd]
    )
    grads_core = to_core(grads_two)
    product0, grads = run(
        first_product_kernel,
        [((rows, cols), F32), ((4 * tokens, cols), BF16)],
        [here, from_core, first, far, out_grads, grads_core],
        blocks={0: blocks_of(0, 1), 1: blocks_of(0, 1)},
    )
    got0 = to_place(product0, 1)
    crossed12 = cross(1, 2, [grads_two])
    crossed3 = cross(3, 1, [product0])
    (proj_stack,) = run(
        gather_kernel, [((3, *half_rank), F32)], [proj_mid, proj_odd], after=[product0]
    )
    proj_others = to_island(proj_stack)

    row_block = ((rows, cols), F32)
    (product1,) = run(
        functools.partial(product_kernel, 1, 0),
        [row_block],
        [here, from_core, crossed12, grads],
        after=[proj_stack],
    )
    got1 = to_place(product1, 1)
    product2, sum2 = run(
        product_and_sum_kernel,
        [row_block, row_block],
        [here, from_core, crossed12, grads, got0],
        after=[product1],
    )
    got2 = to_place(sum2, 2)
    inner_sum = total(inner_weights[0], to_island(inner_weights[0]), after=[sum2])
    (product3,) = run(
        functools.partial(product_kernel, 3, 0),
        [row_block],
        [here, from_core, crossed3, grads],
        after=[inner_sum],
    )

    (partial,) = run(
        lift_kernel,
        [((rank, cols), F32)],
        [flag, product0, product1, product2, product3, projection, proj_stack, proj_others],
    )

    def double(value, bit, exchange):
        other = exchange(value)
        return jnp.where(
            bit == 0,
            jnp.concatenate([value, other]),
            jnp.concatenate([other, value]),
        )

    def halves(value, bit):
        half = value.shape[0] // 2
        low, high = value[:half], value[half:]
        return jnp.where(bit == 0, low, high), jnp.where(bit == 0, high, low)

    quarter_rows = rank // 4
    number = 2 * core + side

    def quarter_of(which):
        return lax.select_n(
            which,
            *(partial[q * quarter_rows : (q + 1) * quarter_rows] for q in range(4)),
        )

    terms = [
        quarter_of(number),
        to_far(quarter_of(number ^ 3)),
        to_side(quarter_of(number ^ 1)),
        to_core(quarter_of(number ^ 2)),
    ]
    partial = total(*terms)
    partial_next = to_place(partial, 1)
    grad_rows = total(product3, got1, got2, after=[partial])
    grad_other = to_island(grad_rows)
    partial = total(partial, partial_next, after=[got1, got2])
    partial_next = to_place(partial, 2)
    partial = total(partial, partial_next)
    partial = double(partial, side, to_side)
    token = to_core(grad_other[: rank // 4])
    projected = double(partial, core, to_core)
    (scale,) = run(
        scale_kernel,
        [((1, cols), F32)],
        [projected, first_moment[0, 0], second_moment[0, 0]],
        after=[token],
    )

    new_first, new_second, _ = moments_and_scale(
        projected, first_moment[0, 0], second_moment[0, 0]
    )
    scale_other = to_island(scale)
    weights_block, new_momentum = run(
        outer_kernel,
        [((rows, cols // 2), BF16), ((rows, cols), F32)],
        [flag, inner_sum, grad_rows, grad_other, scale, scale_other, global_weights, outer_momentum],
    )
    return (weights_block, new_momentum, new_first[None, None], new_second[None, None])


def solution(mesh):
    placed = (
        P("island", "fsdp", None),
        P("island", "fsdp", None),
        P("fsdp", None),
        P("island", None, None, None),
        P("island", None, None, None),
        P("island", "fsdp", None),
        P("fsdp", None),
        P("fsdp", None),
    )
    lined = mesh.shape["fsdp"] == 4 * 4 and mesh.shape["island"] == 2
    return jax.shard_map(
        line_body if lined else plain_body,
        mesh=mesh,
        in_specs=placed,
        out_specs=(
            P("fsdp", "island"),
            P("fsdp", None),
            P("island", None, None, None),
            P("island", None, None, None),
        ),
        check_vma=False,
    )
```

```python
import functools

import jax
import jax.numpy as jnp
from jax import lax
from jax.experimental import pallas as pl
from jax.experimental.pallas import tpu as pltpu
from jax.sharding import PartitionSpec as P

first_decay = 0.9
second_decay = 0.999
first_fix = 1.0 - 0.9**10
second_fix = 1.0 - 0.999**10
epsilon = 1e-08
inner_rate = 1.0
outer_rate = 0.7
outer_beta = 0.9


def outer_step(stepped_sum, global_part, momentum_part, island_count):
    pseudo_grad = global_part - stepped_sum / island_count
    momentum_next = outer_beta * momentum_part + pseudo_grad
    weights_next = (global_part - outer_rate * (pseudo_grad + outer_beta * momentum_next)).astype(
        jnp.bfloat16
    )
    return (weights_next, momentum_next)


def moments_and_scale(projected, first, second):
    new_first = first_decay * first + (1.0 - first_decay) * projected
    new_second = second_decay * second + (1.0 - second_decay) * projected * projected
    adapted = new_first / first_fix / (jnp.sqrt(new_second / second_fix) + epsilon)
    scale = jnp.sqrt(jnp.mean(adapted * adapted, axis=0, keepdims=True)) / jnp.sqrt(
        jnp.mean(projected * projected, axis=0, keepdims=True) + 1e-06
    )
    return new_first, new_second, scale


def plain_body(
    activations,
    out_grads,
    projection,
    first_moment,
    second_moment,
    inner_weights,
    global_weights,
    outer_momentum,
):
    col_total = global_weights.shape[1]
    product = lax.dot_general(
        activations[0],
        out_grads[0],
        (((0,), (0,)), ((), ())),
        preferred_element_type=jnp.float32,
    )
    grad_rows = lax.psum_scatter(product, "fsdp", scatter_dimension=0, tiled=True)
    partial_sum = lax.dot_general(
        projection.astype(jnp.float32),
        grad_rows,
        (((0,), (0,)), ((), ())),
        precision=lax.Precision.HIGHEST,
        preferred_element_type=jnp.float32,
    )
    projected = lax.psum(partial_sum, "fsdp")
    new_first, new_second, scale = moments_and_scale(
        projected, first_moment[0, 0], second_moment[0, 0]
    )
    stepped = inner_weights[0] - inner_rate * grad_rows * scale
    island_count = lax.axis_size("island")
    block_cols = col_total // island_count
    block_start = lax.axis_index("island") * block_cols
    share_total = lax.psum_scatter(stepped, "island", scatter_dimension=1, tiled=True)
    global_part = lax.dynamic_slice_in_dim(global_weights, block_start, block_cols, 1)
    momentum_part = lax.dynamic_slice_in_dim(outer_momentum, block_start, block_cols, 1)
    weights_block, momentum_block = outer_step(
        share_total, global_part, momentum_part, island_count
    )
    new_momentum = lax.all_gather(momentum_block, "island", axis=1, tiled=True)
    return (weights_block, new_momentum, new_first[None, None], new_second[None, None])


VMEM_BYTES = 16 * 1024 * 1024


def whole_block(shape):
    return pl.BlockSpec(shape, lambda *_: (0,) * len(shape))


def run(kernel, out_shapes, args, after=(), scalars=None, blocks=None, scratch=()):
    blocks = blocks or {}
    lead = 0 if scalars is None else 1
    ins = lead + len(args)

    def body(*refs):
        kernel(*refs[:ins], *refs[ins + len(after) :])

    return pl.pallas_call(
        body,
        out_shape=[jax.ShapeDtypeStruct(shape, kind) for shape, kind in out_shapes],
        grid_spec=pltpu.PrefetchScalarGridSpec(
            num_scalar_prefetch=lead,
            grid=(1,),
            in_specs=[blocks.get(i, whole_block(arg.shape)) for i, arg in enumerate(args)]
            + [pl.BlockSpec(memory_space=pl.ANY)] * len(after),
            out_specs=[whole_block(shape) for shape, _ in out_shapes],
            scratch_shapes=scratch,
        ),
        compiler_params=pltpu.CompilerParams(vmem_limit_bytes=VMEM_BYTES),
        cost_estimate=pl.CostEstimate(flops=0, bytes_accessed=0, transcendentals=0),
    )(*(() if scalars is None else (scalars,)), *args, *after)


F32 = jnp.float32
BF16 = jnp.bfloat16


def turn_kernel(at, a_ref, g_ref, first, far, rest, here, cores, passed, turned):
    tokens, features = a_ref.shape[1:]
    cols = g_ref.shape[2]
    line, rows = here.shape[:2]
    for at_col in range(0, features, tokens):
        turned[at_col : at_col + tokens, :] = (
            a_ref[0, :, at_col : at_col + tokens].astype(F32).T
        )
    for at_col in range(0, cols, tokens):
        first[at_col : at_col + tokens, :] = g_ref[0, :, at_col : at_col + tokens].astype(F32)
    side, core = at[line], at[line + 1]

    def block(k, toward, which):
        start = pl.multiple_of(((at[k] * 2 + toward) * 2 + which) * rows, 8)
        return turned[pl.ds(start, rows), :]

    first[cols:, :] = block(0, 1 - side, core)
    far[...] = block(0, 1 - side, 1 - core)
    for k in range(line):
        here[k] = block(k, side, core)
        cores[k] = block(k, side, 1 - core)
        if k:
            rest[k - 1] = block(k, 1 - side, core)
            passed[k - 1] = block(k, 1 - side, 1 - core)


def pair_kernel(*refs):
    out = refs[-1]
    for i, ref in enumerate(refs[:-1]):
        out[i % 2, i // 2] = ref[...]


def stack_kernel(*refs):
    for i, ref in enumerate(refs[:-1]):
        refs[-1][i] = ref[...]


def gather_kernel(mid, odd, out):
    out[0] = odd[0]
    out[1] = mid[...]
    out[2] = odd[1]


def half_kernel(flag, value, out):
    half = out.shape[1]
    out[...] = jnp.where(
        flag[:, :half] == 0, value[:, :half].astype(F32), value[:, half:].astype(F32)
    )


def two_kernel(g_ref, crossed, out):
    tokens = g_ref.shape[1]
    cols = g_ref.shape[2]
    for at_col in range(0, cols, tokens):
        out[0, at_col : at_col + tokens, :] = g_ref[0, :, at_col : at_col + tokens].astype(F32)
    out[1] = crossed[:cols, :]


def first_product_kernel(here, core_a, crossed, far, g_ref, core_g, out, grads):
    tokens = g_ref.shape[1]
    cols = g_ref.shape[2]
    grads[:tokens, :] = g_ref[0]
    for at_col in range(0, cols, tokens):
        span = slice(at_col, at_col + tokens)
        grads[tokens : 2 * tokens, span] = core_g[0, span, :].astype(BF16)
        grads[2 * tokens : 3 * tokens, span] = crossed[span, :].astype(BF16)
        grads[3 * tokens :, span] = core_g[1, span, :].astype(BF16)
    pieces = (here[0], core_a[0], crossed[cols:, :], far[...])
    a = jnp.concatenate([piece.astype(BF16) for piece in pieces], axis=1)
    out[...] = jnp.dot(a, grads[...], preferred_element_type=F32)


def later_product(k, i, here, core_a, crossed, grads):
    pieces = (here[k], core_a[k], crossed[0, i], crossed[1, i])
    a = jnp.concatenate([piece.astype(BF16) for piece in pieces], axis=1)
    return jnp.dot(a, grads[...], preferred_element_type=F32)


def product_kernel(k, i, here, core_a, crossed, grads, out):
    out[...] = later_product(k, i, here, core_a, crossed, grads)


def product_and_sum_kernel(here, core_a, crossed, grads, got, out, out_sum):
    product = later_product(2, 1, here, core_a, crossed, grads)
    out[...] = product
    out_sum[...] = product + got[...]


def sum_kernel(*refs):
    total = refs[0][...]
    for ref in refs[1:-1]:
        total = total + ref[...]
    refs[-1][...] = total


def lift_kernel(flag, p0, p1, p2, p3, own, received, others, out):
    half = others.shape[2]
    first = flag[:, :half] == 0
    low, high = own[:, :half].astype(F32), own[:, half:].astype(F32)
    mine = (received[2], received[0], received[1], jnp.where(first, low, high))
    theirs = (others[2], others[0], others[1], jnp.where(first, high, low))
    splits = []
    for product in (p0, p1, p2, p3):
        value = product[...]
        top = value.astype(BF16)
        splits.append((top, (value - top.astype(F32)).astype(BF16)))
    totals = []
    for rows in (mine, theirs):
        total = None
        for row, parts in zip(rows, splits):
            turned = row.T.astype(BF16)
            for part in parts:
                term = jnp.dot(turned, part, preferred_element_type=F32)
                total = term if total is None else total + term
        totals.append(total)
    first = flag[...] == 0
    out[:half, :] = jnp.where(first, totals[0], totals[1])
    out[half:, :] = jnp.where(first, totals[1], totals[0])


def scale_kernel(projected, first, second, out):
    _, _, out[...] = moments_and_scale(projected[...], first[...], second[...])


def outer_kernel(
    flag, inner_sum, grad, grad_other, scale, scale_other, weights, momentum, out, momentum_out
):
    first_island = flag[...] == 0
    own, other = grad[...] * scale[...], grad_other[...] * scale_other[...]
    first, second = jnp.where(first_island, own, other), jnp.where(first_island, other, own)
    total = (inner_sum[...] - inner_rate * first) - inner_rate * second
    weights_next, momentum_next = outer_step(total, weights[...], momentum[...], 2)
    half = out.shape[1]
    out[...] = jnp.where(
        flag[:, :half] == 0,
        weights_next[:, :half].astype(F32),
        weights_next[:, half:].astype(F32),
    ).astype(BF16)
    momentum_out[...] = momentum_next


def line_body(
    activations,
    out_grads,
    projection,
    first_moment,
    second_moment,
    inner_weights,
    global_weights,
    outer_momentum,
):
    fsdp = lax.axis_size("fsdp")
    line = fsdp // 4
    me = lax.axis_index("fsdp")
    place, side, core = me // 4, (me // 2) % 2, me % 2
    rows = projection.shape[0]
    tokens, features = activations.shape[1:]
    cols = global_weights.shape[1]
    rank = projection.shape[1]

    def move(value, target):
        pairs = []
        for f in range(fsdp):
            to = target(f // 4, (f // 2) % 2, f % 2)
            if to is not None:
                pairs.append((f, (to[0] * 2 + to[1]) * 2 + to[2]))
        return lax.ppermute(value, "fsdp", pairs)

    def to_core(value):
        return move(value, lambda l, x, c: (l, x, 1 - c))

    def to_side(value):
        return move(value, lambda l, x, c: (l, 1 - x, c))

    def to_far(value):
        return move(value, lambda l, x, c: (l, 1 - x, 1 - c))

    def to_place(value, mask):
        return move(value, lambda l, x, c: (l ^ mask, x, c))

    def to_island(value):
        return lax.ppermute(value, "island", [(0, 1), (1, 0)])

    island = lax.axis_index("island")
    at = jnp.stack([place ^ 3, place ^ 1, place ^ 2, place, side, core]).astype(jnp.int32)
    flag = jnp.full((1, cols), island, F32)

    block_shape = (rows, tokens)
    first, far, rest, here, cores, passed = run(
        turn_kernel,
        [
            ((cols + rows, tokens), F32),
            (block_shape, F32),
            ((line - 1, *block_shape), F32),
            ((line, *block_shape), F32),
            ((line, *block_shape), F32),
            ((line - 1, *block_shape), F32),
        ],
        [activations, out_grads],
        scalars=at,
        scratch=[pltpu.VMEM((features, tokens), F32)],
    )
    first = to_side(first)
    far = to_far(far)
    from_core = to_core(cores)
    passed = to_core(passed)

    def blocks_of(start, count):
        return pl.BlockSpec((count, *block_shape), lambda *_: (start // count, 0, 0))

    def cross(k, count, after):
        parts = []
        for i in range(count):
            parts += [rest[k - 1 + i], passed[k - 1 + i]]
        (paired,) = run(
            pair_kernel, [((2, count, *block_shape), F32)], parts, after=after
        )
        return to_side(paired)

    def total(*terms, after=()):
        return run(sum_kernel, [(terms[0].shape, F32)], terms, after=after)[0]

    half_rank = (rows, rank // 2)
    (proj_half,) = run(half_kernel, [(half_rank, F32)], [flag, projection])
    proj_mid = to_place(proj_half, 2)
    (proj_two,) = run(stack_kernel, [((2, *half_rank), F32)], [proj_half, proj_mid])
    proj_odd = to_place(proj_two, 1)
    (grads_two,) = run(
        two_kernel, [((2, cols, tokens), F32)], [out_grads, first], after=[far, proj_odd]
    )
    grads_core = to_core(grads_two)
    product0, grads = run(
        first_product_kernel,
        [((rows, cols), F32), ((4 * tokens, cols), BF16)],
        [here, from_core, first, far, out_grads, grads_core],
        blocks={0: blocks_of(0, 1), 1: blocks_of(0, 1)},
    )
    got0 = to_place(product0, 1)
    crossed12 = cross(1, 2, [grads_two])
    crossed3 = cross(3, 1, [product0])
    (proj_stack,) = run(
        gather_kernel, [((3, *half_rank), F32)], [proj_mid, proj_odd], after=[product0]
    )
    proj_others = to_island(proj_stack)

    row_block = ((rows, cols), F32)
    (product1,) = run(
        functools.partial(product_kernel, 1, 0),
        [row_block],
        [here, from_core, crossed12, grads],
        after=[proj_stack],
    )
    got1 = to_place(product1, 1)
    product2, sum2 = run(
        product_and_sum_kernel,
        [row_block, row_block],
        [here, from_core, crossed12, grads, got0],
        after=[product1],
    )
    got2 = to_place(sum2, 2)
    inner_sum = total(inner_weights[0], to_island(inner_weights[0]), after=[sum2])
    (product3,) = run(
        functools.partial(product_kernel, 3, 0),
        [row_block],
        [here, from_core, crossed3, grads],
        after=[inner_sum],
    )

    (partial,) = run(
        lift_kernel,
        [((rank, cols), F32)],
        [flag, product0, product1, product2, product3, projection, proj_stack, proj_others],
    )

    def double(value, bit, exchange):
        other = exchange(value)
        return jnp.where(
            bit == 0,
            jnp.concatenate([value, other]),
            jnp.concatenate([other, value]),
        )

    def halves(value, bit):
        half = value.shape[0] // 2
        low, high = value[:half], value[half:]
        return jnp.where(bit == 0, low, high), jnp.where(bit == 0, high, low)

    quarter_rows = rank // 4
    number = 2 * core + side

    def quarter_of(which):
        return lax.select_n(
            which,
            *(partial[q * quarter_rows : (q + 1) * quarter_rows] for q in range(4)),
        )

    terms = [
        quarter_of(number),
        to_far(quarter_of(number ^ 3)),
        to_side(quarter_of(number ^ 1)),
        to_core(quarter_of(number ^ 2)),
    ]
    partial = total(*terms)
    partial_next = to_place(partial, 1)
    grad_rows = total(product3, got1, got2, after=[partial])
    grad_other = to_island(grad_rows)
    partial = total(partial, partial_next, after=[got1, got2])
    partial_next = to_place(partial, 2)
    partial = total(partial, partial_next)
    partial = double(partial, side, to_side)
    token = to_core(grad_other[: rank // 16])
    projected = double(partial, core, to_core)
    (scale,) = run(
        scale_kernel,
        [((1, cols), F32)],
        [projected, first_moment[0, 0], second_moment[0, 0]],
        after=[token],
    )

    new_first, new_second, _ = moments_and_scale(
        projected, first_moment[0, 0], second_moment[0, 0]
    )
    scale_other = to_island(scale)
    weights_block, new_momentum = run(
        outer_kernel,
        [((rows, cols // 2), BF16), ((rows, cols), F32)],
        [flag, inner_sum, grad_rows, grad_other, scale, scale_other, global_weights, outer_momentum],
    )
    return (weights_block, new_momentum, new_first[None, None], new_second[None, None])


def solution(mesh):
    placed = (
        P("island", "fsdp", None),
        P("island", "fsdp", None),
        P("fsdp", None),
        P("island", None, None, None),
        P("island", None, None, None),
        P("island", "fsdp", None),
        P("fsdp", None),
        P("fsdp", None),
    )
    lined = mesh.shape["fsdp"] == 4 * 4 and mesh.shape["island"] == 2
    return jax.shard_map(
        line_body if lined else plain_body,
        mesh=mesh,
        in_specs=placed,
        out_specs=(
            P("fsdp", "island"),
            P("fsdp", None),
            P("island", None, None, None),
            P("island", None, None, None),
        ),
        check_vma=False,
    )
```
